32 devices in a mesh: tile: 8 (over y, x, core), lev: 4 (over z).
Axes of the slice: x: 2, y: 2, z: 4, core: 2. Of those that a mesh axis runs over, the one named last changes fastest.
Arguments:
- tracers: float32 [8, 8, 8, 72, 128], P('tile', None, None, 'lev'), may hold values from -6 to 6
- courant_first: float32 [8, 8, 8, 72], P('tile', None, None, 'lev'), may hold values from -0.9 to 0.9
- courant_second: float32 [8, 8, 8, 72], P('tile', None, None, 'lev'), may hold values from -0.9 to 0.9
- weights: float32 [8, 8, 8, 72, 72], P('tile', 'lev'), may hold values from 0.05 to 1
- frame_flip: int32 [8, 2], P('tile'), may hold values from 0 to 1
Outputs:
- transported: float32 [8, 8, 8, 72, 128], P('tile', None, None, 'lev')
The draws below stay inside these ranges and needn't reach their ends.
All inputs are finite; a program needn't handle non-finite values.
Results may differ from the reference program's by a relative error of at most 0.0003.
Values sent between devices are 32-bit elements; how exact they have to be, the bound alone decides.
No kernel may reach another device: no remote copies, remote signals or barrier semaphores. Data moves between devices by JAX's collectives and lax.ppermute only.
A program may use at most 64 MiB of HBM per device.

```python
import jax
import jax.numpy as jnp
from jax import lax

SIDE = 8
LEVELS = 72
TRACERS = 128
SUBSTEPS = 3
TILES = 8
STRIDE = 2


def set_ends(result, rng, least, high):
    index_at = [jax.random.randint(jax.random.fold_in(rng, axis), (), 0, length) for axis, length in enumerate(result.shape)]
    widest = result.shape.index(max(result.shape))
    beside = index_at[:widest] + [(index_at[widest] + 1) % result.shape[widest]] + index_at[widest + 1:]
    return result.at[tuple(index_at)].set(least).at[tuple(beside)].set(high)


def block_levels(own_key, dims, split, low, high):
    def one(dim, shards_of):
        heights = jax.random.uniform(jax.random.fold_in(jax.random.fold_in(own_key, 6), dim), (shards_of,), jnp.float32, low / len(split), high / len(split))
        return jnp.repeat(jnp.exp(heights), dims[dim] // shards_of).reshape((-1,) + (1,) * (len(dims) - dim - 1))

    gain = one(*split[0])
    for cut in split[1:]:
        gain = gain * one(*cut)
    return gain


def gaussian(stream_key, extent, spread, reach, cuts=(), kind=jnp.bfloat16):
    level = block_levels(stream_key, extent, cuts, -0.22, 0.18) if cuts else 1.0
    array = jax.random.normal(stream_key, extent, jnp.float32) * spread * level
    return jnp.minimum(jnp.maximum(array, -reach), reach).astype(kind)


def setup_inputs(seed: int = 0) -> dict:
    key_of = jax.random.split(jax.random.key(seed), 6)
    return {
        "tracers": gaussian(key_of[0], (TILES, SIDE, SIDE, LEVELS, TRACERS), 1.0, 6.0, ((0, 8), (3, 4)), jnp.float32),
        "courant_first": jnp.clip(jax.random.uniform(key_of[1], (TILES, SIDE, SIDE, LEVELS), jnp.float32, -0.9, 0.9) * block_levels(key_of[1], (TILES, SIDE, SIDE, LEVELS), ((0, 8), (3, 4)), -0.4, 0.0), -0.9, 0.9),
        "courant_second": jnp.clip(jax.random.uniform(key_of[2], (TILES, SIDE, SIDE, LEVELS), jnp.float32, -0.9, 0.9) * block_levels(key_of[2], (TILES, SIDE, SIDE, LEVELS), ((0, 8), (3, 4)), -0.4, 0.0), -0.9, 0.9),
        "weights": jnp.clip(0.05 + 0.95 * jax.random.uniform(key_of[3], (TILES, SIDE, SIDE, LEVELS, LEVELS), jnp.float32) ** block_levels(key_of[3], (TILES, SIDE, SIDE, LEVELS, LEVELS), ((0, 8), (1, 4)), -0.2, 0.2), 0.05, 1.0),
        "frame_flip": set_ends(jax.random.randint(key_of[4], (TILES, 2), 0, 2), jax.random.fold_in(key_of[4], 1), 0, 1).astype(jnp.int32),
    }


group_width = 16


def ppm_update(extended, courant, along):
    length = extended.shape[along] - 6

    def window(values, offset, amount):
        return lax.slice_in_dim(values, offset, offset + amount, axis=along)

    interfaces = (7.0 * (window(extended, 1, length + 3) + window(extended, 2, length + 3)) - (window(extended, 0, length + 3) + window(extended, 3, length + 3))) / 12.0
    low_edge = window(interfaces, 0, length + 2)
    high_edge = window(interfaces, 1, length + 2)
    centre = window(extended, 2, length + 2)
    gradient = high_edge - low_edge
    curvature = 6.0 * centre - 3.0 * (low_edge + high_edge)
    upward = courant * (window(high_edge, 0, length + 1) - 0.5 * courant * (window(gradient, 0, length + 1) - (1.0 - courant * (2.0 / 3.0)) * window(curvature, 0, length + 1)))
    downward = courant * (window(low_edge, 1, length + 1) - 0.5 * courant * (window(gradient, 1, length + 1) + (1.0 + courant * (2.0 / 3.0)) * window(curvature, 1, length + 1)))
    fluxes = jnp.where(courant >= 0.0, upward, downward)
    return window(centre, 1, length) - (window(fluxes, 1, length) - window(fluxes, 0, length))


def to_frame(blocks, flip_flags):
    first_flag = (flip_flags[:, 0] == 1)[:, None, None, None, None]
    second_flag = (flip_flags[:, 1] == 1)[:, None, None, None, None]
    turned = jnp.where(first_flag, blocks[:, ::-1], blocks)
    return jnp.where(second_flag, turned[:, :, ::-1], turned)


def mixing_matrix(weights):
    totals = jnp.sum(weights, axis=-1, keepdims=True)
    identity = jnp.eye(weights.shape[-1], dtype=jnp.float32)
    return 0.6 * identity + 0.4 * (weights / totals)


def reference(tracers, courant_first, courant_second, weights, frame_flip):
    mixing = mixing_matrix(weights)
    first_faces = jnp.concatenate([jnp.roll(courant_first, STRIDE, axis=0)[:, SIDE - 1:], courant_first], axis=1)[..., None]
    second_faces = jnp.concatenate([jnp.roll(courant_second, 1, axis=0)[:, :, SIDE - 1:], courant_second], axis=2)[..., None]

    def advance(blocks):
        fields = to_frame(blocks, frame_flip)
        for substep in range(SUBSTEPS):
            extended = jnp.concatenate([jnp.roll(fields, STRIDE, axis=0)[:, SIDE - 3:], fields, jnp.roll(fields, -STRIDE, axis=0)[:, :3]], axis=1)
            fields = ppm_update(extended, first_faces, 1)
            extended = jnp.concatenate([jnp.roll(fields, 1, axis=0)[:, :, SIDE - 3:], fields, jnp.roll(fields, -1, axis=0)[:, :, :3]], axis=2)
            fields = ppm_update(extended, second_faces, 2)
        advected = to_frame(fields, frame_flip)
        return jnp.einsum("txykl,txylq->txykq", mixing, advected, precision=lax.Precision.HIGHEST)

    grouped = tracers.reshape(TILES, SIDE, SIDE, LEVELS, TRACERS // group_width, group_width)
    grouped = jnp.moveaxis(grouped, 4, 0)
    results = lax.map(advance, grouped)
    return jnp.moveaxis(results, 0, 4).reshape(TILES, SIDE, SIDE, LEVELS, TRACERS)
```

```python
import functools

import jax
import jax.numpy as jnp
from jax import lax
from jax.experimental import pallas as pl
from jax.experimental.pallas import tpu as pltpu
from jax.sharding import PartitionSpec as P

SUBSTEPS = 3
SUBLANES = 8
LANES = 128
VMEM_LIMIT = 40 * 1024 * 1024


def passed_along(value, axis, steps):
    count = lax.axis_size(axis)
    pairs = [(source, (source + steps) % count) for source in range(count)]
    return lax.ppermute(value, axis, pairs)


def ppm_update(extended, courant, along):
    length = extended.shape[along] - 6

    def window(values, offset, amount):
        return lax.slice_in_dim(values, offset, offset + amount, axis=along)

    interfaces = (
        7.0 * (window(extended, 1, length + 3) + window(extended, 2, length + 3))
        - (window(extended, 0, length + 3) + window(extended, 3, length + 3))
    ) / 12.0
    low_edge = window(interfaces, 0, length + 2)
    high_edge = window(interfaces, 1, length + 2)
    centre = window(extended, 2, length + 2)
    gradient = high_edge - low_edge
    curvature = 6.0 * centre - 3.0 * (low_edge + high_edge)
    upward = courant * (
        window(high_edge, 0, length + 1)
        - 0.5
        * courant
        * (
            window(gradient, 0, length + 1)
            - (1.0 - courant * (2.0 / 3.0)) * window(curvature, 0, length + 1)
        )
    )
    downward = courant * (
        window(low_edge, 1, length + 1)
        - 0.5
        * courant
        * (
            window(gradient, 1, length + 1)
            + (1.0 + courant * (2.0 / 3.0)) * window(curvature, 1, length + 1)
        )
    )
    fluxes = jnp.where(courant >= 0.0, upward, downward)
    return window(centre, 1, length) - (window(fluxes, 1, length) - window(fluxes, 0, length))


def to_frame(blocks, flip_flags):
    first_flag = (flip_flags[:, 0] == 1)[:, None, None, None, None]
    second_flag = (flip_flags[:, 1] == 1)[:, None, None, None, None]
    turned = jnp.where(first_flag, blocks[:, ::-1], blocks)
    return jnp.where(second_flag, turned[:, :, ::-1], turned)


def mixing_matrix(weights):
    totals = jnp.sum(weights, axis=-1, keepdims=True)
    identity = jnp.eye(weights.shape[-1], dtype=jnp.float32)
    return 0.6 * identity + 0.4 * (weights / totals)


def tile_stride(tiles):
    return max(2, tiles // 8)


def by_halos(tracers, courant_first, courant_second, weights, frame_flip):
    stride = tile_stride(lax.axis_size("tile"))
    extent = tracers.shape[1]
    fields = to_frame(tracers, frame_flip)
    first_faces = courant_first[..., None]
    second_faces = courant_second[..., None]
    for substep in range(SUBSTEPS):
        for along, faces, steps in ((1, first_faces, stride), (2, second_faces, 1)):
            size = fields.shape[along]
            high_cells = lax.slice_in_dim(fields, size - 3, size, axis=along)
            low_cells = lax.slice_in_dim(fields, 0, 3, axis=along)
            high_face = lax.slice_in_dim(faces, size - 1, size, axis=along)
            from_low, low_face = passed_along((high_cells, high_face), "tile", steps)
            from_high = passed_along(low_cells, "tile", -steps)
            fields = ppm_update(
                jnp.concatenate([from_low, fields, from_high], axis=along),
                jnp.concatenate([low_face, faces], axis=along),
                along,
            )
    advected = to_frame(fields, frame_flip)
    mixing = mixing_matrix(weights)
    columns = lax.all_to_all(advected, "lev", split_axis=1, concat_axis=3, tiled=True)
    mixed = jnp.einsum("txykl,txylq->txykq", mixing, columns, precision=lax.Precision.HIGHEST)
    return lax.all_to_all(mixed, "lev", split_axis=3, concat_axis=1, tiled=True)


class Plan:
    def __init__(self, side, levels, tracers, tiles, layers):
        self.side, self.levels, self.tracers = side, levels, tracers
        self.tiles, self.layers = tiles, layers
        self.cells = side * side
        self.full = levels // tiles
        self.spare = levels - self.full * tiles
        self.fits = (
            tiles == SUBLANES
            and tracers == LANES
            and self.cells * 2 == LANES
            and side % layers == 0
            and self.spare > 0
            and self.full > 0
            and tiles % self.spare == 0
        )
        if not self.fits:
            return
        self.groups = tiles // self.spare
        self.width = tracers // self.groups
        self.part_rows = self.cells // self.groups
        self.kinds = self.full + 1
        self.tail_at = self.full * self.cells
        self.courant_at = self.tail_at + self.part_rows
        self.flip_at = self.courant_at + self.kinds
        self.rows = -(-(self.flip_at + 1) // SUBLANES) * SUBLANES
        self.own_cells = self.cells // layers
        self.back_tail = self.full * self.own_cells
        self.back_part = self.own_cells // self.groups
        self.back_rows = -(-(self.back_tail + self.back_part) // SUBLANES) * SUBLANES
        self.all_levels = levels * layers
        self.fits = (
            self.cells % self.groups == 0
            and self.own_cells % self.groups == 0
            and self.part_rows % SUBLANES == 0
        )


def lane_group(shape, width):
    return lax.broadcasted_iota(jnp.int32, shape, 1) // width


def pack_kernel(p, x_ref, first_ref, second_ref, flip_ref, out_ref, spare_ref, faces_ref, sems):
    copies = []
    for d in range(p.tiles):
        for f in range(p.full):
            copies.append(
                pltpu.make_async_copy(
                    x_ref.at[:, p.full * d + f, :],
                    out_ref.at[d, pl.ds(f * p.cells, p.cells), :],
                    sems.at[len(copies)],
                )
            )
    spares = []
    for h in range(p.spare):
        spares.append(
            pltpu.make_async_copy(
                x_ref.at[:, p.full * p.tiles + h, :],
                spare_ref.at[h],
                sems.at[len(copies) + h],
            )
        )
    for copy in spares + copies:
        copy.start()
    faces_ref[...] = jnp.zeros_like(faces_ref)
    faces_ref[: p.cells, : p.levels] = first_ref[...]
    faces_ref[p.cells :, : p.levels] = second_ref[...]
    faces = faces_ref[...].T
    lane = lax.broadcasted_iota(jnp.int32, (1, LANES), 1)
    first_flip = jnp.full((1, LANES), flip_ref[0, 0]).astype(jnp.float32)
    second_flip = jnp.full((1, LANES), flip_ref[0, 1]).astype(jnp.float32)
    flips = jnp.where(lane < p.cells, first_flip, second_flip)
    filler = jnp.zeros((p.rows - p.flip_at - 1, LANES), jnp.float32)
    for d in range(p.tiles):
        level = p.full * d
        out_ref[d, p.courant_at : p.courant_at + p.full, :] = faces[level : level + p.full]
        rest = p.full * p.tiles + d // p.groups
        out_ref[d, p.courant_at + p.full : p.flip_at, :] = faces[rest : rest + 1]
        out_ref[d, p.flip_at : p.flip_at + 1, :] = flips
        if p.rows > p.flip_at + 1:
            out_ref[d, p.flip_at + 1 :, :] = filler
    for copy in spares:
        copy.wait()
    group = lane_group((p.part_rows, LANES), p.width)
    for h in range(p.spare):
        parts = [spare_ref[h, m * p.part_rows : (m + 1) * p.part_rows, :] for m in range(p.groups)]
        for g in range(p.groups):
            rows = None
            for m in range(p.groups):
                shift = (m - g) * p.width % LANES
                moved = pltpu.roll(parts[m], shift, 1) if shift else parts[m]
                rows = moved if rows is None else jnp.where(group == m, moved, rows)
            out_ref[h * p.groups + g, p.tail_at : p.tail_at + p.part_rows, :] = rows
    for copy in copies:
        copy.wait()


def advect_kernel(p, stride, in_ref, out_ref, q_ref, near_ref, far_ref, mid_ref):
    tiles, side, cells = p.tiles, p.side, p.cells
    shape = (tiles, LANES)

    def row(at):
        return in_ref[pl.ds(at, tiles, stride=p.rows), :]

    flips = row(p.flip_at)
    first_flip = jnp.broadcast_to(flips[:, 0:1], shape) > 0.5
    second_flip = jnp.broadcast_to(flips[:, cells : cells + 1], shape) > 0.5

    def turned(get):
        for i in range(side // 2):
            for j in range(side // 2):
                i2, j2 = side - 1 - i, side - 1 - j
                ll, hl, lh, hh = get(i, j), get(i2, j), get(i, j2), get(i2, j2)
                a, b = jnp.where(first_flip, hl, ll), jnp.where(first_flip, ll, hl)
                c, d = jnp.where(first_flip, hh, lh), jnp.where(first_flip, lh, hh)
                yield i * side + j, jnp.where(second_flip, c, a)
                yield i2 * side + j, jnp.where(second_flip, d, b)
                yield i * side + j2, jnp.where(second_flip, a, c)
                yield i2 * side + j2, jnp.where(second_flip, b, d)

    for kind in range(p.kinds):
        if kind < p.full:
            get = lambda i, j: row(kind * cells + i * side + j)
        else:

            def get(i, j):
                m, r = divmod(i * side + j, p.part_rows)
                value = row(p.tail_at + r)
                return pltpu.roll(value, LANES - m * p.width, 1) if m else value

        for cell, value in turned(get):
            q_ref[kind * cells + cell] = value
        courant = row(p.courant_at + kind)
        for at in range(2 * cells):
            c = jnp.broadcast_to(courant[:, at : at + 1], shape)
            e = jnp.abs(c)
            u = 1.0 - e
            cu = c * u
            near_ref[kind * 2 * cells + at] = (cu * u) * (1.0 / 12.0)
            far_ref[kind * 2 * cells + at] = (cu * e) * (-1.0 / 12.0)
            mid_ref[kind * 2 * cells + at] = (c * e) * (3.0 - 2.0 * e)

    def sweep(at, faces_at, step, shift):
        cell = [at + step * i for i in range(side)]
        face = [faces_at + step * i for i in range(side)]
        q = [q_ref[cell[i]] for i in range(side)]
        up = lambda v: pltpu.roll(v, shift, 0)
        down = lambda v: pltpu.roll(v, tiles - shift, 0)
        ext = [up(q[side - 1])] + q + [down(q[0]), down(q[1])]
        edge = [
            7.0 * (ext[i + 1] + ext[i + 2]) - (ext[i] + ext[i + 3]) for i in range(side)
        ]
        edges = [up(edge[side - 1])] + edge + [down(edge[0])]
        flux = []
        for i in range(side):
            near = near_ref[face[i]]
            upwind = near >= 0.0
            far = jnp.where(upwind, edges[i], edges[i + 2])
            mid = jnp.where(upwind, ext[i + 1], ext[i + 2])
            flux.append(near * edge[i] + far_ref[face[i]] * far + mid_ref[face[i]] * mid)
        fluxes = [up(flux[side - 1])] + flux
        for i in range(side):
            q_ref[cell[i]] = q[i] - (fluxes[i + 1] - fluxes[i])

    def step(count, carry):
        kind = count // SUBSTEPS
        at = kind * cells
        faces_at = kind * 2 * cells
        for j in range(side):
            sweep(at + j, faces_at + j, side, stride)
        for i in range(side):
            sweep(at + i * side, faces_at + cells + i * side, 1, 1)
        return carry

    lax.fori_loop(0, p.kinds * SUBSTEPS, step, 0)

    pitch = p.layers * p.back_rows

    def send(cell_layer, at, value):
        out_ref[pl.ds(cell_layer * p.back_rows + at, tiles, stride=pitch), :] = value

    for kind in range(p.kinds):
        back = turned(lambda i, j: q_ref[kind * cells + i * side + j])
        if kind < p.full:
            for cell, value in back:
                layer, own = divmod(cell, p.own_cells)
                send(layer, kind * p.own_cells + own, value)
        else:
            for cell, value in back:
                q_ref[kind * cells + cell] = value
    group = lane_group(shape, p.width)
    for layer in range(p.layers):
        for r in range(p.back_part):
            rows = None
            for m in range(p.groups):
                value = q_ref[p.full * cells + layer * p.own_cells + m * p.back_part + r]
                moved = pltpu.roll(value, m * p.width, 1) if m else value
                rows = moved if rows is None else jnp.where(group == m, moved, rows)
            send(layer, p.back_tail + r, rows)


def mix_kernel(p, in_ref, weights_ref, *refs):
    out_refs, (x_ref, all_ref) = refs[: p.layers], refs[p.layers :]
    tiles = p.tiles
    shape = (tiles, LANES)
    pitch = p.layers * p.back_rows
    group = lane_group(shape, p.width)
    part = lax.broadcasted_iota(jnp.int32, shape, 0) % p.groups
    places = [(group == g) & (part == g) for g in range(p.groups)]

    def row(layer, at):
        return in_ref[pl.ds(layer * p.back_rows + at, tiles, stride=pitch), :]

    for r in range(p.back_part):
        turned = []
        for layer in range(p.layers):
            value = row(layer, p.back_tail + r)
            turned.append([value] + [pltpu.roll(value, s * p.width, 1) for s in range(1, p.groups)])
        for m in range(p.groups):
            own = m * p.back_part + r
            for layer in range(p.layers):
                base = layer * p.levels
                for f in range(p.full):
                    x_ref[own, pl.ds(base + f, tiles, stride=p.full), :] = row(
                        layer, f * p.own_cells + own
                    )
                tail = jnp.zeros(shape, jnp.float32)
                for g in range(p.groups):
                    tail = jnp.where(places[g], turned[layer][(g - m) % p.groups], tail)
                reach = 1
                while reach < p.groups:
                    tail = tail + pltpu.roll(tail, tiles - reach, 0)
                    reach *= 2
                for h in range(p.spare):
                    at = base + p.full * tiles + h
                    x_ref[own, at : at + 1, :] = tail[h * p.groups : h * p.groups + 1]
    for own in range(p.own_cells):
        x = x_ref[own]
        weights = weights_ref[own]
        scale = 0.4 / jnp.sum(weights, axis=-1, keepdims=True)
        x_high = x.astype(jnp.bfloat16)
        x_low = (x - x_high.astype(jnp.float32)).astype(jnp.bfloat16)
        w_high = weights.astype(jnp.bfloat16)
        w_low = (weights - w_high.astype(jnp.float32)).astype(jnp.bfloat16)
        dot = functools.partial(jnp.dot, preferred_element_type=jnp.float32)
        total = dot(w_high, x_high) + (dot(w_high, x_low) + dot(w_low, x_high))
        all_ref[pl.ds(own, p.all_levels, stride=p.own_cells), :] = 0.6 * x + scale * total
    me = lax.axis_index("lev")
    size = p.levels * p.own_cells
    for s in range(p.layers):
        layer = lax.rem(me + s, p.layers)
        out_refs[s][...] = all_ref[pl.ds(pl.multiple_of(layer * size, SUBLANES), size), :]


def place_kernel(p, *refs):
    in_refs, out_ref = refs[: p.layers], refs[p.layers]
    me = lax.axis_index("lev")
    for s in range(p.layers):
        layer = lax.rem(me - s + p.layers, p.layers)
        for own in range(p.own_cells):
            out_ref[layer * p.own_cells + own] = in_refs[s][
                pl.ds(own, p.levels, stride=p.own_cells), :
            ]


def in_vmem(count):
    return [pl.BlockSpec(memory_space=pltpu.VMEM)] * count


def params():
    return pltpu.CompilerParams(vmem_limit_bytes=VMEM_LIMIT)


def by_levels(p, tracers, courant_first, courant_second, weights, frame_flip):
    f32 = jnp.float32
    copies = p.tiles * p.full + p.spare
    packed = pl.pallas_call(
        functools.partial(pack_kernel, p),
        out_shape=jax.ShapeDtypeStruct((p.tiles, p.rows, LANES), f32),
        in_specs=[pl.BlockSpec(memory_space=pl.ANY)]
        + in_vmem(2)
        + [pl.BlockSpec(memory_space=pltpu.SMEM)],
        out_specs=pl.BlockSpec(memory_space=pltpu.VMEM),
        scratch_shapes=[
            pltpu.VMEM((p.spare, p.cells, LANES), f32),
            pltpu.VMEM((LANES, LANES), f32),
            pltpu.SemaphoreType.DMA((copies,)),
        ],
        compiler_params=params(),
        name="pack",
    )(
        tracers.reshape(p.cells, p.levels, p.tracers),
        courant_first.reshape(p.cells, p.levels),
        courant_second.reshape(p.cells, p.levels),
        frame_flip,
    )
    dealt = lax.all_to_all(packed, "tile", split_axis=0, concat_axis=0, tiled=True)
    moved = pl.pallas_call(
        functools.partial(advect_kernel, p, tile_stride(p.tiles)),
        out_shape=jax.ShapeDtypeStruct((p.tiles * p.layers * p.back_rows, LANES), f32),
        in_specs=in_vmem(1),
        out_specs=pl.BlockSpec(memory_space=pltpu.VMEM),
        scratch_shapes=[pltpu.VMEM((p.kinds * p.cells, p.tiles, LANES), f32)]
        + [pltpu.VMEM((p.kinds * 2 * p.cells, p.tiles, LANES), f32)] * 3,
        compiler_params=params(),
        name="advect",
    )(dealt.reshape(p.tiles * p.rows, LANES))
    columns = lax.all_to_all(
        moved.reshape(p.tiles * p.layers, p.back_rows, LANES),
        ("tile", "lev"),
        split_axis=0,
        concat_axis=0,
        tiled=True,
    )
    size = p.levels * p.own_cells
    mixed = pl.pallas_call(
        functools.partial(mix_kernel, p),
        out_shape=[jax.ShapeDtypeStruct((size, LANES), f32)] * p.layers,
        in_specs=in_vmem(2),
        out_specs=in_vmem(p.layers),
        scratch_shapes=[
            pltpu.VMEM((p.own_cells, p.all_levels, LANES), f32),
            pltpu.VMEM((p.all_levels * p.own_cells, LANES), f32),
        ],
        compiler_params=params(),
        name="mix",
    )(
        columns.reshape(p.tiles * p.layers * p.back_rows, LANES),
        weights.reshape(p.own_cells, p.all_levels, p.all_levels),
    )
    pieces = [mixed[0]] + [passed_along(mixed[s], "lev", s) for s in range(1, p.layers)]
    placed = pl.pallas_call(
        functools.partial(place_kernel, p),
        out_shape=jax.ShapeDtypeStruct((p.cells, p.levels, LANES), f32),
        in_specs=in_vmem(p.layers),
        out_specs=pl.BlockSpec(memory_space=pltpu.VMEM),
        compiler_params=params(),
        name="place",
    )(*pieces)
    return placed.reshape(tracers.shape)


def on_device(tracers, courant_first, courant_second, weights, frame_flip):
    plan = Plan(
        tracers.shape[1],
        tracers.shape[3],
        tracers.shape[4],
        lax.axis_size("tile"),
        lax.axis_size("lev"),
    )
    if tracers.shape[1] == tracers.shape[2] and tracers.shape[0] == 1 and plan.fits:
        return by_levels(plan, tracers, courant_first, courant_second, weights, frame_flip)
    return by_halos(tracers, courant_first, courant_second, weights, frame_flip)


def solution(mesh):
    in_specs = (
        P("tile", None, None, "lev", None),
        P("tile", None, None, "lev"),
        P("tile", None, None, "lev"),
        P("tile", "lev", None, None, None),
        P("tile", None),
    )
    out_specs = P("tile", None, None, "lev", None)
    return jax.shard_map(
        on_device, mesh=mesh, in_specs=in_specs, out_specs=out_specs, check_vma=False
    )
```

```python
import functools

import jax
import jax.numpy as jnp
from jax import lax
from jax.experimental import pallas as pl
from jax.experimental.pallas import tpu as pltpu
from jax.sharding import PartitionSpec as P

SUBSTEPS = 3
SUBLANES = 8
LANES = 128
VMEM_LIMIT = 40 * 1024 * 1024


def passed_along(value, axis, steps):
    count = lax.axis_size(axis)
    pairs = [(source, (source + steps) % count) for source in range(count)]
    return lax.ppermute(value, axis, pairs)


def ppm_update(extended, courant, along):
    length = extended.shape[along] - 6

    def window(values, offset, amount):
        return lax.slice_in_dim(values, offset, offset + amount, axis=along)

    interfaces = (
        7.0 * (window(extended, 1, length + 3) + window(extended, 2, length + 3))
        - (window(extended, 0, length + 3) + window(extended, 3, length + 3))
    ) / 12.0
    low_edge = window(interfaces, 0, length + 2)
    high_edge = window(interfaces, 1, length + 2)
    centre = window(extended, 2, length + 2)
    gradient = high_edge - low_edge
    curvature = 6.0 * centre - 3.0 * (low_edge + high_edge)
    upward = courant * (
        window(high_edge, 0, length + 1)
        - 0.5
        * courant
        * (
            window(gradient, 0, length + 1)
            - (1.0 - courant * (2.0 / 3.0)) * window(curvature, 0, length + 1)
        )
    )
    downward = courant * (
        window(low_edge, 1, length + 1)
        - 0.5
        * courant
        * (
            window(gradient, 1, length + 1)
            + (1.0 + courant * (2.0 / 3.0)) * window(curvature, 1, length + 1)
        )
    )
    fluxes = jnp.where(courant >= 0.0, upward, downward)
    return window(centre, 1, length) - (window(fluxes, 1, length) - window(fluxes, 0, length))


def to_frame(blocks, flip_flags):
    first_flag = (flip_flags[:, 0] == 1)[:, None, None, None, None]
    second_flag = (flip_flags[:, 1] == 1)[:, None, None, None, None]
    turned = jnp.where(first_flag, blocks[:, ::-1], blocks)
    return jnp.where(second_flag, turned[:, :, ::-1], turned)


def mixing_matrix(weights):
    totals = jnp.sum(weights, axis=-1, keepdims=True)
    identity = jnp.eye(weights.shape[-1], dtype=jnp.float32)
    return 0.6 * identity + 0.4 * (weights / totals)


def tile_stride(tiles):
    return max(2, tiles // 8)


def by_halos(tracers, courant_first, courant_second, weights, frame_flip):
    stride = tile_stride(lax.axis_size("tile"))
    extent = tracers.shape[1]
    fields = to_frame(tracers, frame_flip)
    first_faces = courant_first[..., None]
    second_faces = courant_second[..., None]
    for substep in range(SUBSTEPS):
        for along, faces, steps in ((1, first_faces, stride), (2, second_faces, 1)):
            size = fields.shape[along]
            high_cells = lax.slice_in_dim(fields, size - 3, size, axis=along)
            low_cells = lax.slice_in_dim(fields, 0, 3, axis=along)
            high_face = lax.slice_in_dim(faces, size - 1, size, axis=along)
            from_low, low_face = passed_along((high_cells, high_face), "tile", steps)
            from_high = passed_along(low_cells, "tile", -steps)
            fields = ppm_update(
                jnp.concatenate([from_low, fields, from_high], axis=along),
                jnp.concatenate([low_face, faces], axis=along),
                along,
            )
    advected = to_frame(fields, frame_flip)
    mixing = mixing_matrix(weights)
    columns = lax.all_to_all(advected, "lev", split_axis=1, concat_axis=3, tiled=True)
    mixed = jnp.einsum("txykl,txylq->txykq", mixing, columns, precision=lax.Precision.HIGHEST)
    return lax.all_to_all(mixed, "lev", split_axis=3, concat_axis=1, tiled=True)


class Plan:
    def __init__(self, side, levels, tracers, tiles, layers):
        self.side, self.levels, self.tracers = side, levels, tracers
        self.tiles, self.layers = tiles, layers
        self.cells = side * side
        self.full = levels // tiles
        self.spare = levels - self.full * tiles
        self.fits = (
            tiles == SUBLANES
            and tracers == LANES
            and self.cells * 2 == LANES
            and side % layers == 0
            and self.spare > 0
            and self.full > 0
            and tiles % self.spare == 0
        )
        if not self.fits:
            return
        self.groups = tiles // self.spare
        self.width = tracers // self.groups
        self.part_rows = self.cells // self.groups
        self.kinds = self.full + 1
        self.tail_at = self.full * self.cells
        self.courant_at = self.tail_at + self.part_rows
        self.flip_at = self.courant_at + self.kinds
        self.rows = -(-(self.flip_at + 1) // SUBLANES) * SUBLANES
        self.own_cells = self.cells // layers
        self.back_tail = self.full * self.own_cells
        self.back_part = self.own_cells // self.groups
        self.back_rows = -(-(self.back_tail + self.back_part) // SUBLANES) * SUBLANES
        self.all_levels = levels * layers
        self.fits = (
            self.cells % self.groups == 0
            and self.own_cells % self.groups == 0
            and self.part_rows % SUBLANES == 0
            and self.side == SUBLANES
            and self.own_cells % side == 0
            and self.kinds < SUBLANES
        )


def lane_group(shape, width):
    return lax.broadcasted_iota(jnp.int32, shape, 1) // width


def pack_kernel(
    p, x_ref, first_ref, second_ref, flip_ref, out_ref, spare_ref, courant_ref, flags_ref, faces_ref, sems
):
    copies = []

    def fetch(source, target):
        copy = pltpu.make_async_copy(source, target, sems.at[len(copies)])
        copy.start()
        copies.append(copy)

    for source, target in ((first_ref, courant_ref.at[0]), (second_ref, courant_ref.at[1])):
        fetch(source, target)
    fetch(flip_ref, flags_ref)
    for h in range(p.spare):
        fetch(x_ref.at[:, p.full * p.tiles + h], spare_ref.at[h])
    small = 3
    for d in range(p.tiles):
        for f in range(p.full):
            fetch(
                x_ref.at[:, p.full * d + f],
                out_ref.at[d, pl.ds(f * p.side, p.side)],
            )
    filler = jnp.zeros((p.side, LANES), jnp.float32)
    group = lane_group((p.side, LANES), p.width)
    for copy in copies[small : small + p.spare]:
        copy.wait()
    tall = p.part_rows // p.side
    for h in range(p.spare):
        for g in range(p.groups):
            for r in range(tall):
                rows = None
                for m in range(p.groups):
                    part = spare_ref[h, m * tall + r]
                    shift = (m - g) * p.width % LANES
                    moved = pltpu.roll(part, shift, 1) if shift else part
                    rows = moved if rows is None else jnp.where(group == m, moved, rows)
                out_ref[h * p.groups + g, p.full * p.side + r] = rows
    for copy in copies[:small]:
        copy.wait()
    for way in range(2):
        for i in range(p.side):
            at = way * p.cells + i * p.side
            faces_ref[at : at + p.side, :] = filler
            faces_ref[at : at + p.side, : p.levels] = courant_ref[way, i]
    faces = faces_ref[...].T
    lane = lax.broadcasted_iota(jnp.int32, (1, LANES), 1)
    flags = flags_ref[...].astype(jnp.float32)
    flips = jnp.where(
        lane < p.cells,
        jnp.broadcast_to(flags[:, 0:1], (1, LANES)),
        jnp.broadcast_to(flags[:, 1:2], (1, LANES)),
    )
    last = p.courant_at // SUBLANES
    for d in range(p.tiles):
        level = p.full * d
        rest = p.full * p.tiles + d // p.groups
        out_ref[d, last] = filler
        out_ref[d, last, : p.full, :] = faces[level : level + p.full]
        out_ref[d, last, p.full : p.kinds, :] = faces[rest : rest + 1]
        out_ref[d, last, p.kinds : p.kinds + 1, :] = flips
    for copy in copies[small + p.spare :]:
        copy.wait()


def advect_kernel(p, stride, in_ref, out_ref, q_ref, near_ref, far_ref, mid_ref):
    tiles, side, cells = p.tiles, p.side, p.cells
    shape = (tiles, LANES)

    def row(at):
        return in_ref[pl.ds(at, tiles, stride=p.rows), :]

    flips = row(p.flip_at)
    first_flip = jnp.broadcast_to(flips[:, 0:1], shape) > 0.5
    second_flip = jnp.broadcast_to(flips[:, cells : cells + 1], shape) > 0.5

    def turned(get):
        for i in range(side // 2):
            for j in range(side // 2):
                i2, j2 = side - 1 - i, side - 1 - j
                ll, hl, lh, hh = get(i, j), get(i2, j), get(i, j2), get(i2, j2)
                a, b = jnp.where(first_flip, hl, ll), jnp.where(first_flip, ll, hl)
                c, d = jnp.where(first_flip, hh, lh), jnp.where(first_flip, lh, hh)
                yield i * side + j, jnp.where(second_flip, c, a)
                yield i2 * side + j, jnp.where(second_flip, d, b)
                yield i * side + j2, jnp.where(second_flip, a, c)
                yield i2 * side + j2, jnp.where(second_flip, b, d)

    for kind in range(p.kinds):
        if kind < p.full:
            get = lambda i, j: row(kind * cells + i * side + j)
        else:

            def get(i, j):
                m, r = divmod(i * side + j, p.part_rows)
                value = row(p.tail_at + r)
                return pltpu.roll(value, LANES - m * p.width, 1) if m else value

        for cell, value in turned(get):
            q_ref[kind * cells + cell] = value
        courant = row(p.courant_at + kind)
        for at in range(2 * cells):
            c = jnp.broadcast_to(courant[:, at : at + 1], shape)
            e = jnp.abs(c)
            u = 1.0 - e
            cu = c * u
            near_ref[kind * 2 * cells + at] = (cu * u) * (1.0 / 12.0)
            far_ref[kind * 2 * cells + at] = (cu * e) * (-1.0 / 12.0)
            mid_ref[kind * 2 * cells + at] = (c * e) * (3.0 - 2.0 * e)

    def sweep(at, faces_at, step, shift):
        cell = [at + step * i for i in range(side)]
        face = [faces_at + step * i for i in range(side)]
        q = [q_ref[cell[i]] for i in range(side)]
        up = lambda v: pltpu.roll(v, shift, 0)
        down = lambda v: pltpu.roll(v, tiles - shift, 0)
        ext = [up(q[side - 1])] + q + [down(q[0]), down(q[1])]
        edge = [
            7.0 * (ext[i + 1] + ext[i + 2]) - (ext[i] + ext[i + 3]) for i in range(side)
        ]
        edges = [up(edge[side - 1])] + edge + [down(edge[0])]
        flux = []
        for i in range(side):
            near = near_ref[face[i]]
            upwind = near >= 0.0
            far = jnp.where(upwind, edges[i], edges[i + 2])
            mid = jnp.where(upwind, ext[i + 1], ext[i + 2])
            flux.append(near * edge[i] + far_ref[face[i]] * far + mid_ref[face[i]] * mid)
        fluxes = [up(flux[side - 1])] + flux
        for i in range(side):
            q_ref[cell[i]] = q[i] - (fluxes[i + 1] - fluxes[i])

    def step(count, carry):
        kind = count // SUBSTEPS
        at = kind * cells
        faces_at = kind * 2 * cells
        for j in range(side):
            sweep(at + j, faces_at + j, side, stride)
        for i in range(side):
            sweep(at + i * side, faces_at + cells + i * side, 1, 1)
        return carry

    lax.fori_loop(0, p.kinds * SUBSTEPS, step, 0)

    pitch = p.layers * p.back_rows

    def send(cell_layer, at, value):
        out_ref[pl.ds(cell_layer * p.back_rows + at, tiles, stride=pitch), :] = value

    for kind in range(p.kinds):
        back = turned(lambda i, j: q_ref[kind * cells + i * side + j])
        if kind < p.full:
            for cell, value in back:
                layer, own = divmod(cell, p.own_cells)
                send(layer, kind * p.own_cells + own, value)
        else:
            for cell, value in back:
                q_ref[kind * cells + cell] = value
    group = lane_group(shape, p.width)
    for layer in range(p.layers):
        for r in range(p.back_part):
            rows = None
            for m in range(p.groups):
                value = q_ref[p.full * cells + layer * p.own_cells + m * p.back_part + r]
                moved = pltpu.roll(value, m * p.width, 1) if m else value
                rows = moved if rows is None else jnp.where(group == m, moved, rows)
            send(layer, p.back_tail + r, rows)


def mix_kernel(p, in_ref, weights_ref, *refs):
    out_refs, (x_ref, all_ref) = refs[: p.layers], refs[p.layers :]
    tiles = p.tiles
    shape = (tiles, LANES)
    pitch = p.layers * p.back_rows
    group = lane_group(shape, p.width)
    part = lax.broadcasted_iota(jnp.int32, shape, 0) % p.groups
    places = [(group == g) & (part == g) for g in range(p.groups)]

    def row(layer, at):
        return in_ref[pl.ds(layer * p.back_rows + at, tiles, stride=pitch), :]

    for r in range(p.back_part):
        turned = []
        for layer in range(p.layers):
            value = row(layer, p.back_tail + r)
            turned.append([value] + [pltpu.roll(value, s * p.width, 1) for s in range(1, p.groups)])
        for m in range(p.groups):
            own = m * p.back_part + r
            for layer in range(p.layers):
                base = layer * p.levels
                for f in range(p.full):
                    x_ref[own, pl.ds(base + f, tiles, stride=p.full), :] = row(
                        layer, f * p.own_cells + own
                    )
                tail = jnp.zeros(shape, jnp.float32)
                for g in range(p.groups):
                    tail = jnp.where(places[g], turned[layer][(g - m) % p.groups], tail)
                reach = 1
                while reach < p.groups:
                    tail = tail + pltpu.roll(tail, tiles - reach, 0)
                    reach *= 2
                for h in range(p.spare):
                    at = base + p.full * tiles + h
                    x_ref[own, at : at + 1, :] = tail[h * p.groups : h * p.groups + 1]
    for own in range(p.own_cells):
        x = x_ref[own]
        weights = weights_ref[own]
        scale = 0.4 / jnp.sum(weights, axis=-1, keepdims=True)
        x_high = x.astype(jnp.bfloat16)
        x_low = (x - x_high.astype(jnp.float32)).astype(jnp.bfloat16)
        w_high = weights.astype(jnp.bfloat16)
        w_low = (weights - w_high.astype(jnp.float32)).astype(jnp.bfloat16)
        dot = functools.partial(jnp.dot, preferred_element_type=jnp.float32)
        total = dot(w_high, x_high) + (dot(w_high, x_low) + dot(w_low, x_high))
        all_ref[pl.ds(own, p.all_levels, stride=p.own_cells), :] = 0.6 * x + scale * total
    me = lax.axis_index("lev")
    size = p.levels * p.own_cells
    for s in range(p.layers):
        layer = lax.rem(me + s, p.layers)
        out_refs[s][...] = all_ref[pl.ds(pl.multiple_of(layer * size, SUBLANES), size), :]


def place_kernel(p, *refs):
    in_refs, out_ref = refs[: p.layers], refs[p.layers]
    me = lax.axis_index("lev")
    tall = p.own_cells // p.side
    for s in range(p.layers):
        layer = lax.rem(me - s + p.layers, p.layers)
        for level in range(p.levels):
            for r in range(tall):
                at = level * p.own_cells + r * p.side
                out_ref[layer * tall + r, level] = in_refs[s][at : at + p.side, :]


def in_vmem(count):
    return [pl.BlockSpec(memory_space=pltpu.VMEM)] * count


def params():
    return pltpu.CompilerParams(vmem_limit_bytes=VMEM_LIMIT)


def by_levels(p, tracers, courant_first, courant_second, weights, frame_flip):
    f32 = jnp.float32
    across = (p.side, p.levels, p.side, p.tracers)
    packed = pl.pallas_call(
        functools.partial(pack_kernel, p),
        out_shape=jax.ShapeDtypeStruct((p.tiles, p.rows // p.side, p.side, LANES), f32),
        in_specs=[pl.BlockSpec(memory_space=pltpu.HBM)] * 4,
        out_specs=pl.BlockSpec(memory_space=pltpu.VMEM),
        scratch_shapes=[
            pltpu.VMEM((p.spare, p.side, p.side, LANES), f32),
            pltpu.VMEM((2, p.side, p.side, p.levels), f32),
            pltpu.VMEM((1, 2), jnp.int32),
            pltpu.VMEM((LANES, LANES), f32),
            pltpu.SemaphoreType.DMA((3 + p.tiles * p.full + p.spare,)),
        ],
        compiler_params=params(),
        name="pack",
    )(
        *(
            pltpu.with_memory_space_constraint(value, pltpu.HBM)
            for value in (
                tracers[0].transpose(0, 2, 1, 3),
                courant_first[0],
                courant_second[0],
                frame_flip,
            )
        )
    )
    dealt = lax.all_to_all(packed, "tile", split_axis=0, concat_axis=0, tiled=True)
    moved = pl.pallas_call(
        functools.partial(advect_kernel, p, tile_stride(p.tiles)),
        out_shape=jax.ShapeDtypeStruct((p.tiles * p.layers * p.back_rows, LANES), f32),
        in_specs=in_vmem(1),
        out_specs=pl.BlockSpec(memory_space=pltpu.VMEM),
        scratch_shapes=[pltpu.VMEM((p.kinds * p.cells, p.tiles, LANES), f32)]
        + [pltpu.VMEM((p.kinds * 2 * p.cells, p.tiles, LANES), f32)] * 3,
        compiler_params=params(),
        name="advect",
    )(dealt.reshape(p.tiles * p.rows, LANES))
    columns = lax.all_to_all(
        moved.reshape(p.tiles * p.layers, p.back_rows, LANES),
        ("tile", "lev"),
        split_axis=0,
        concat_axis=0,
        tiled=True,
    )
    size = p.levels * p.own_cells
    mixed = pl.pallas_call(
        functools.partial(mix_kernel, p),
        out_shape=[jax.ShapeDtypeStruct((size, LANES), f32)] * p.layers,
        in_specs=in_vmem(2),
        out_specs=in_vmem(p.layers),
        scratch_shapes=[
            pltpu.VMEM((p.own_cells, p.all_levels, LANES), f32),
            pltpu.VMEM((p.all_levels * p.own_cells, LANES), f32),
        ],
        compiler_params=params(),
        name="mix",
    )(
        columns.reshape(p.tiles * p.layers * p.back_rows, LANES),
        weights.reshape(p.own_cells, p.all_levels, p.all_levels),
    )
    pieces = [mixed[0]] + [passed_along(mixed[s], "lev", s) for s in range(1, p.layers)]
    placed = pl.pallas_call(
        functools.partial(place_kernel, p),
        out_shape=jax.ShapeDtypeStruct(across, f32),
        in_specs=in_vmem(p.layers),
        out_specs=pl.BlockSpec(memory_space=pltpu.VMEM),
        compiler_params=params(),
        name="place",
    )(*pieces)
    return placed.transpose(0, 2, 1, 3)[None]


def on_device(tracers, courant_first, courant_second, weights, frame_flip):
    plan = Plan(
        tracers.shape[1],
        tracers.shape[3],
        tracers.shape[4],
        lax.axis_size("tile"),
        lax.axis_size("lev"),
    )
    if tracers.shape[1] == tracers.shape[2] and tracers.shape[0] == 1 and plan.fits:
        return by_levels(plan, tracers, courant_first, courant_second, weights, frame_flip)
    return by_halos(tracers, courant_first, courant_second, weights, frame_flip)


def solution(mesh):
    in_specs = (
        P("tile", None, None, "lev", None),
        P("tile", None, None, "lev"),
        P("tile", None, None, "lev"),
        P("tile", "lev", None, None, None),
        P("tile", None),
    )
    out_specs = P("tile", None, None, "lev", None)
    return jax.shard_map(
        on_device, mesh=mesh, in_specs=in_specs, out_specs=out_specs, check_vma=False
    )
```

```python
import functools

import jax
import jax.numpy as jnp
from jax import lax
from jax.experimental import pallas as pl
from jax.experimental.pallas import tpu as pltpu
from jax.sharding import PartitionSpec as P

SUBSTEPS = 3
SUBLANES = 8
LANES = 128
VMEM_LIMIT = 40 * 1024 * 1024


def passed_along(value, axis, steps):
    count = lax.axis_size(axis)
    pairs = [(source, (source + steps) % count) for source in range(count)]
    return lax.ppermute(value, axis, pairs)


def ppm_update(extended, courant, along):
    length = extended.shape[along] - 6

    def window(values, offset, amount):
        return lax.slice_in_dim(values, offset, offset + amount, axis=along)

    interfaces = (
        7.0 * (window(extended, 1, length + 3) + window(extended, 2, length + 3))
        - (window(extended, 0, length + 3) + window(extended, 3, length + 3))
    ) / 12.0
    low_edge = window(interfaces, 0, length + 2)
    high_edge = window(interfaces, 1, length + 2)
    centre = window(extended, 2, length + 2)
    gradient = high_edge - low_edge
    curvature = 6.0 * centre - 3.0 * (low_edge + high_edge)
    upward = courant * (
        window(high_edge, 0, length + 1)
        - 0.5
        * courant
        * (
            window(gradient, 0, length + 1)
            - (1.0 - courant * (2.0 / 3.0)) * window(curvature, 0, length + 1)
        )
    )
    downward = courant * (
        window(low_edge, 1, length + 1)
        - 0.5
        * courant
        * (
            window(gradient, 1, length + 1)
            + (1.0 + courant * (2.0 / 3.0)) * window(curvature, 1, length + 1)
        )
    )
    fluxes = jnp.where(courant >= 0.0, upward, downward)
    return window(centre, 1, length) - (window(fluxes, 1, length) - window(fluxes, 0, length))


def to_frame(blocks, flip_flags):
    first_flag = (flip_flags[:, 0] == 1)[:, None, None, None, None]
    second_flag = (flip_flags[:, 1] == 1)[:, None, None, None, None]
    turned = jnp.where(first_flag, blocks[:, ::-1], blocks)
    return jnp.where(second_flag, turned[:, :, ::-1], turned)


def mixing_matrix(weights):
    totals = jnp.sum(weights, axis=-1, keepdims=True)
    identity = jnp.eye(weights.shape[-1], dtype=jnp.float32)
    return 0.6 * identity + 0.4 * (weights / totals)


def swapped(value, axis, mask):
    pairs = [(source, source ^ mask) for source in range(lax.axis_size(axis))]
    return lax.ppermute(value, axis, pairs)


def tile_stride(tiles):
    return max(2, tiles // 8)


def by_halos(tracers, courant_first, courant_second, weights, frame_flip):
    stride = tile_stride(lax.axis_size("tile"))
    extent = tracers.shape[1]
    fields = to_frame(tracers, frame_flip)
    first_faces = courant_first[..., None]
    second_faces = courant_second[..., None]
    for substep in range(SUBSTEPS):
        for along, faces, steps in ((1, first_faces, stride), (2, second_faces, 1)):
            size = fields.shape[along]
            high_cells = lax.slice_in_dim(fields, size - 3, size, axis=along)
            low_cells = lax.slice_in_dim(fields, 0, 3, axis=along)
            high_face = lax.slice_in_dim(faces, size - 1, size, axis=along)
            from_low, low_face = passed_along((high_cells, high_face), "tile", steps)
            from_high = passed_along(low_cells, "tile", -steps)
            fields = ppm_update(
                jnp.concatenate([from_low, fields, from_high], axis=along),
                jnp.concatenate([low_face, faces], axis=along),
                along,
            )
    advected = to_frame(fields, frame_flip)
    mixing = mixing_matrix(weights)
    columns = lax.all_to_all(advected, "lev", split_axis=1, concat_axis=3, tiled=True)
    mixed = jnp.einsum("txykl,txylq->txykq", mixing, columns, precision=lax.Precision.HIGHEST)
    return lax.all_to_all(mixed, "lev", split_axis=3, concat_axis=1, tiled=True)


class Plan:
    def __init__(self, side, levels, tracers, tiles, layers):
        self.side, self.levels, self.tracers = side, levels, tracers
        self.tiles, self.layers = tiles, layers
        self.cells = side * side
        self.full = levels // tiles
        self.spare = levels - self.full * tiles
        self.fits = (
            tiles == SUBLANES
            and tracers == LANES
            and self.cells * 2 == LANES
            and side % layers == 0
            and self.spare > 0
            and self.full > 0
            and tiles % self.spare == 0
        )
        if not self.fits:
            return
        self.groups = tiles // self.spare
        self.width = tracers // self.groups
        self.part_rows = self.cells // self.groups
        self.kinds = self.full + 1
        self.tail_at = self.full * self.cells
        self.courant_at = self.tail_at + self.part_rows
        self.flip_at = self.courant_at + self.kinds
        self.rows = -(-(self.flip_at + 1) // SUBLANES) * SUBLANES
        self.own_cells = self.cells // layers
        self.back_tail = self.full * self.own_cells
        self.back_part = self.own_cells // self.groups
        self.back_rows = -(-(self.back_tail + self.back_part) // SUBLANES) * SUBLANES
        self.all_levels = levels * layers
        self.fits = (
            self.cells % self.groups == 0
            and self.own_cells % self.groups == 0
            and self.part_rows % SUBLANES == 0
            and self.side == SUBLANES
            and self.own_cells % side == 0
            and self.kinds < SUBLANES
        )


def lane_group(shape, width):
    return lax.broadcasted_iota(jnp.int32, shape, 1) // width


def pack_kernel(p, x_ref, first_ref, second_ref, flip_ref, *refs):
    chips = p.tiles // 2
    own_refs, other_ref = refs[:chips], refs[chips]
    spare_ref, courant_ref, flags_ref, faces_ref, rest_ref, sems = refs[chips + 1 :]
    me = lax.axis_index("tile")
    slots = []
    for s in range(chips):
        slots.append((lax.bitwise_xor(me, 2 * s), own_refs[s]))
        slots.append((lax.bitwise_xor(me, 2 * s + 1), other_ref.at[s]))
    copies = []

    def fetch(source, target):
        copy = pltpu.make_async_copy(source, target, sems.at[len(copies)])
        copy.start()
        copies.append(copy)

    for source, target in ((first_ref, courant_ref.at[0]), (second_ref, courant_ref.at[1])):
        fetch(source, target)
    fetch(flip_ref, flags_ref)
    for h in range(p.spare):
        fetch(x_ref.at[:, p.full * p.tiles + h], spare_ref.at[h])
    small = 3
    for d, slot in slots:
        for f in range(p.full):
            fetch(x_ref.at[:, p.full * d + f], slot.at[pl.ds(f * p.side, p.side)])
    filler = jnp.zeros((p.side, LANES), jnp.float32)
    group = lane_group((p.side, LANES), p.width)
    for copy in copies[small : small + p.spare]:
        copy.wait()
    tall = p.part_rows // p.side
    for h in range(p.spare):
        for g in range(p.groups):
            for r in range(tall):
                rows = None
                for m in range(p.groups):
                    part = spare_ref[h, m * tall + r]
                    shift = (m - g) * p.width % LANES
                    moved = pltpu.roll(part, shift, 1) if shift else part
                    rows = moved if rows is None else jnp.where(group == m, moved, rows)
                rest_ref[h * p.groups + g, r] = rows
    for copy in copies[:small]:
        copy.wait()
    for way in range(2):
        for i in range(p.side):
            at = way * p.cells + i * p.side
            faces_ref[at : at + p.side, :] = filler
            faces_ref[at : at + p.side, : p.levels] = courant_ref[way, i]
    faces = faces_ref[...].T
    lane = lax.broadcasted_iota(jnp.int32, (1, LANES), 1)
    flags = flags_ref[...].astype(jnp.float32)
    flips = jnp.where(
        lane < p.cells,
        jnp.broadcast_to(flags[:, 0:1], (1, LANES)),
        jnp.broadcast_to(flags[:, 1:2], (1, LANES)),
    )
    for d in range(p.tiles):
        level = p.full * d
        rest = p.full * p.tiles + d // p.groups
        rest_ref[d, tall] = filler
        rest_ref[d, tall, : p.full, :] = faces[level : level + p.full]
        rest_ref[d, tall, p.full : p.kinds, :] = faces[rest : rest + 1]
        rest_ref[d, tall, p.kinds : p.kinds + 1, :] = flips
    for d, slot in slots:
        for r in range(tall + 1):
            slot[p.full * p.side + r] = rest_ref[d, r]
    for copy in copies[small + p.spare :]:
        copy.wait()


def advect_kernel(p, stride, *refs):
    tiles, side, cells = p.tiles, p.side, p.cells
    shape = (tiles, LANES)
    parts = refs[: -6]
    out_ref, in_ref, q_ref, near_ref, far_ref, mid_ref = refs[-6:]
    me = lax.axis_index("tile")
    each = tiles // len(parts)
    for s, part in enumerate(parts):
        for e in range(each):
            tile = lax.bitwise_xor(me, s * each + e)
            in_ref[pl.ds(pl.multiple_of(tile * p.rows, SUBLANES), p.rows), :] = part[
                e * p.rows : (e + 1) * p.rows, :
            ]

    def row(at):
        return in_ref[pl.ds(at, tiles, stride=p.rows), :]

    flips = row(p.flip_at)
    first_flip = jnp.broadcast_to(flips[:, 0:1], shape) > 0.5
    second_flip = jnp.broadcast_to(flips[:, cells : cells + 1], shape) > 0.5

    def turned(get):
        for i in range(side // 2):
            for j in range(side // 2):
                i2, j2 = side - 1 - i, side - 1 - j
                ll, hl, lh, hh = get(i, j), get(i2, j), get(i, j2), get(i2, j2)
                a, b = jnp.where(first_flip, hl, ll), jnp.where(first_flip, ll, hl)
                c, d = jnp.where(first_flip, hh, lh), jnp.where(first_flip, lh, hh)
                yield i * side + j, jnp.where(second_flip, c, a)
                yield i2 * side + j, jnp.where(second_flip, d, b)
                yield i * side + j2, jnp.where(second_flip, a, c)
                yield i2 * side + j2, jnp.where(second_flip, b, d)

    for kind in range(p.kinds):
        if kind < p.full:
            get = lambda i, j: row(kind * cells + i * side + j)
        else:

            def get(i, j):
                m, r = divmod(i * side + j, p.part_rows)
                value = row(p.tail_at + r)
                return pltpu.roll(value, LANES - m * p.width, 1) if m else value

        for cell, value in turned(get):
            q_ref[kind * cells + cell] = value
        courant = row(p.courant_at + kind)
        for at in range(2 * cells):
            c = jnp.broadcast_to(courant[:, at : at + 1], shape)
            e = jnp.abs(c)
            u = 1.0 - e
            cu = c * u
            near_ref[kind * 2 * cells + at] = (cu * u) * (1.0 / 12.0)
            far_ref[kind * 2 * cells + at] = (cu * e) * (-1.0 / 12.0)
            mid_ref[kind * 2 * cells + at] = (c * e) * (3.0 - 2.0 * e)

    def sweep(at, faces_at, step, shift):
        cell = [at + step * i for i in range(side)]
        face = [faces_at + step * i for i in range(side)]
        q = [q_ref[cell[i]] for i in range(side)]
        up = lambda v: pltpu.roll(v, shift, 0)
        down = lambda v: pltpu.roll(v, tiles - shift, 0)
        ext = [up(q[side - 1])] + q + [down(q[0]), down(q[1])]
        edge = [
            7.0 * (ext[i + 1] + ext[i + 2]) - (ext[i] + ext[i + 3]) for i in range(side)
        ]
        edges = [up(edge[side - 1])] + edge + [down(edge[0])]
        flux = []
        for i in range(side):
            near = near_ref[face[i]]
            upwind = near >= 0.0
            far = jnp.where(upwind, edges[i], edges[i + 2])
            mid = jnp.where(upwind, ext[i + 1], ext[i + 2])
            flux.append(near * edge[i] + far_ref[face[i]] * far + mid_ref[face[i]] * mid)
        fluxes = [up(flux[side - 1])] + flux
        for i in range(side):
            q_ref[cell[i]] = q[i] - (fluxes[i + 1] - fluxes[i])

    def step(count, carry):
        kind = count // SUBSTEPS
        at = kind * cells
        faces_at = kind * 2 * cells
        for j in range(side):
            sweep(at + j, faces_at + j, side, stride)
        for i in range(side):
            sweep(at + i * side, faces_at + cells + i * side, 1, 1)
        return carry

    lax.fori_loop(0, p.kinds * SUBSTEPS, step, 0)

    pitch = p.layers * p.back_rows

    def send(cell_layer, at, value):
        out_ref[pl.ds(cell_layer * p.back_rows + at, tiles, stride=pitch), :] = value

    for kind in range(p.kinds):
        back = turned(lambda i, j: q_ref[kind * cells + i * side + j])
        if kind < p.full:
            for cell, value in back:
                layer, own = divmod(cell, p.own_cells)
                send(layer, kind * p.own_cells + own, value)
        else:
            for cell, value in back:
                q_ref[kind * cells + cell] = value
    group = lane_group(shape, p.width)
    for layer in range(p.layers):
        for r in range(p.back_part):
            rows = None
            for m in range(p.groups):
                value = q_ref[p.full * cells + layer * p.own_cells + m * p.back_part + r]
                moved = pltpu.roll(value, m * p.width, 1) if m else value
                rows = moved if rows is None else jnp.where(group == m, moved, rows)
            send(layer, p.back_tail + r, rows)


def mix_kernel(p, in_ref, weights_ref, *refs):
    out_refs, (x_ref, all_ref) = refs[: p.layers], refs[p.layers :]
    tiles = p.tiles
    shape = (tiles, LANES)
    pitch = p.layers * p.back_rows
    group = lane_group(shape, p.width)
    part = lax.broadcasted_iota(jnp.int32, shape, 0) % p.groups
    places = [(group == g) & (part == g) for g in range(p.groups)]

    def row(layer, at):
        return in_ref[pl.ds(layer * p.back_rows + at, tiles, stride=pitch), :]

    for r in range(p.back_part):
        turned = []
        for layer in range(p.layers):
            value = row(layer, p.back_tail + r)
            turned.append([value] + [pltpu.roll(value, s * p.width, 1) for s in range(1, p.groups)])
        for m in range(p.groups):
            own = m * p.back_part + r
            for layer in range(p.layers):
                base = layer * p.levels
                for f in range(p.full):
                    x_ref[own, pl.ds(base + f, tiles, stride=p.full), :] = row(
                        layer, f * p.own_cells + own
                    )
                tail = jnp.zeros(shape, jnp.float32)
                for g in range(p.groups):
                    tail = jnp.where(places[g], turned[layer][(g - m) % p.groups], tail)
                reach = 1
                while reach < p.groups:
                    tail = tail + pltpu.roll(tail, tiles - reach, 0)
                    reach *= 2
                for h in range(p.spare):
                    at = base + p.full * tiles + h
                    x_ref[own, at : at + 1, :] = tail[h * p.groups : h * p.groups + 1]
    for own in range(p.own_cells):
        x = x_ref[own]
        weights = weights_ref[own]
        scale = 0.4 / jnp.sum(weights, axis=-1, keepdims=True)
        x_high = x.astype(jnp.bfloat16)
        x_low = (x - x_high.astype(jnp.float32)).astype(jnp.bfloat16)
        w_high = weights.astype(jnp.bfloat16)
        w_low = (weights - w_high.astype(jnp.float32)).astype(jnp.bfloat16)
        dot = functools.partial(jnp.dot, preferred_element_type=jnp.float32)
        total = dot(w_high, x_high) + (dot(w_high, x_low) + dot(w_low, x_high))
        all_ref[pl.ds(own, p.all_levels, stride=p.own_cells), :] = 0.6 * x + scale * total
    me = lax.axis_index("lev")
    size = p.levels * p.own_cells
    for s in range(p.layers):
        layer = lax.rem(me + s, p.layers)
        out_refs[s][...] = all_ref[pl.ds(pl.multiple_of(layer * size, SUBLANES), size), :]


def place_kernel(p, *refs):
    in_refs, out_ref = refs[: p.layers], refs[p.layers]
    me = lax.axis_index("lev")
    tall = p.own_cells // p.side
    for s in range(p.layers):
        layer = lax.rem(me - s + p.layers, p.layers)
        for level in range(p.levels):
            for r in range(tall):
                at = level * p.own_cells + r * p.side
                out_ref[layer * tall + r, level] = in_refs[s][at : at + p.side, :]


def in_vmem(count):
    return [pl.BlockSpec(memory_space=pltpu.VMEM)] * count


def params():
    return pltpu.CompilerParams(vmem_limit_bytes=VMEM_LIMIT)


def by_levels(p, tracers, courant_first, courant_second, weights, frame_flip):
    f32 = jnp.float32
    across = (p.side, p.levels, p.side, p.tracers)
    chips = p.tiles // 2
    blocks = (p.rows // p.side, p.side, LANES)
    *own, other = pl.pallas_call(
        functools.partial(pack_kernel, p),
        out_shape=[jax.ShapeDtypeStruct(blocks, f32)] * chips
        + [jax.ShapeDtypeStruct((chips,) + blocks, f32)],
        in_specs=[pl.BlockSpec(memory_space=pltpu.HBM)] * 4,
        out_specs=in_vmem(chips + 1),
        scratch_shapes=[
            pltpu.VMEM((p.spare, p.side, p.side, LANES), f32),
            pltpu.VMEM((2, p.side, p.side, p.levels), f32),
            pltpu.VMEM((1, 2), jnp.int32),
            pltpu.VMEM((LANES, LANES), f32),
            pltpu.VMEM((p.tiles, p.part_rows // p.side + 1, p.side, LANES), f32),
            pltpu.SemaphoreType.DMA((3 + p.tiles * p.full + p.spare,)),
        ],
        compiler_params=params(),
        name="pack",
    )(
        *(
            pltpu.with_memory_space_constraint(value, pltpu.HBM)
            for value in (
                tracers[0].transpose(0, 2, 1, 3),
                courant_first[0],
                courant_second[0],
                frame_flip,
            )
        )
    )
    got = swapped(other, "tile", 1)
    pieces = [None] * p.tiles
    for s in range(chips - 1, -1, -1):
        for e, block in ((0, own[s]), (1, got[s])):
            block = block.reshape(p.rows, LANES)
            pieces[2 * s + e] = swapped(block, "tile", 2 * s) if s else block
    moved = pl.pallas_call(
        functools.partial(advect_kernel, p, tile_stride(p.tiles)),
        out_shape=jax.ShapeDtypeStruct((p.tiles * p.layers * p.back_rows, LANES), f32),
        in_specs=in_vmem(len(pieces)),
        out_specs=pl.BlockSpec(memory_space=pltpu.VMEM),
        scratch_shapes=[
            pltpu.VMEM((p.tiles * p.rows, LANES), f32),
            pltpu.VMEM((p.kinds * p.cells, p.tiles, LANES), f32),
        ]
        + [pltpu.VMEM((p.kinds * 2 * p.cells, p.tiles, LANES), f32)] * 3,
        compiler_params=params(),
        name="advect",
    )(*pieces)
    columns = lax.all_to_all(
        moved.reshape(p.tiles * p.layers, p.back_rows, LANES),
        ("tile", "lev"),
        split_axis=0,
        concat_axis=0,
        tiled=True,
    )
    size = p.levels * p.own_cells
    mixed = pl.pallas_call(
        functools.partial(mix_kernel, p),
        out_shape=[jax.ShapeDtypeStruct((size, LANES), f32)] * p.layers,
        in_specs=in_vmem(2),
        out_specs=in_vmem(p.layers),
        scratch_shapes=[
            pltpu.VMEM((p.own_cells, p.all_levels, LANES), f32),
            pltpu.VMEM((p.all_levels * p.own_cells, LANES), f32),
        ],
        compiler_params=params(),
        name="mix",
    )(
        columns.reshape(p.tiles * p.layers * p.back_rows, LANES),
        weights.reshape(p.own_cells, p.all_levels, p.all_levels),
    )
    pieces = [mixed[0]] + [passed_along(mixed[s], "lev", s) for s in range(1, p.layers)]
    placed = pl.pallas_call(
        functools.partial(place_kernel, p),
        out_shape=jax.ShapeDtypeStruct(across, f32),
        in_specs=in_vmem(p.layers),
        out_specs=pl.BlockSpec(memory_space=pltpu.VMEM),
        compiler_params=params(),
        name="place",
    )(*pieces)
    return placed.transpose(0, 2, 1, 3)[None]


def on_device(tracers, courant_first, courant_second, weights, frame_flip):
    plan = Plan(
        tracers.shape[1],
        tracers.shape[3],
        tracers.shape[4],
        lax.axis_size("tile"),
        lax.axis_size("lev"),
    )
    if tracers.shape[1] == tracers.shape[2] and tracers.shape[0] == 1 and plan.fits:
        return by_levels(plan, tracers, courant_first, courant_second, weights, frame_flip)
    return by_halos(tracers, courant_first, courant_second, weights, frame_flip)


def solution(mesh):
    in_specs = (
        P("tile", None, None, "lev", None),
        P("tile", None, None, "lev"),
        P("tile", None, None, "lev"),
        P("tile", "lev", None, None, None),
        P("tile", None),
    )
    out_specs = P("tile", None, None, "lev", None)
    return jax.shard_map(
        on_device, mesh=mesh, in_specs=in_specs, out_specs=out_specs, check_vma=False
    )
```

```python
import functools

import jax
import jax.numpy as jnp
from jax import lax
from jax.experimental import pallas as pl
from jax.experimental.pallas import tpu as pltpu
from jax.sharding import PartitionSpec as P

SUBSTEPS = 3
SUBLANES = 8
LANES = 128
FEW = 4
VMEM_LIMIT = 40 * 1024 * 1024


def passed_along(value, axis, steps):
    count = lax.axis_size(axis)
    pairs = [(source, (source + steps) % count) for source in range(count)]
    return lax.ppermute(value, axis, pairs)


def ppm_update(extended, courant, along):
    length = extended.shape[along] - 6

    def window(values, offset, amount):
        return lax.slice_in_dim(values, offset, offset + amount, axis=along)

    interfaces = (
        7.0 * (window(extended, 1, length + 3) + window(extended, 2, length + 3))
        - (window(extended, 0, length + 3) + window(extended, 3, length + 3))
    ) / 12.0
    low_edge = window(interfaces, 0, length + 2)
    high_edge = window(interfaces, 1, length + 2)
    centre = window(extended, 2, length + 2)
    gradient = high_edge - low_edge
    curvature = 6.0 * centre - 3.0 * (low_edge + high_edge)
    upward = courant * (
        window(high_edge, 0, length + 1)
        - 0.5
        * courant
        * (
            window(gradient, 0, length + 1)
            - (1.0 - courant * (2.0 / 3.0)) * window(curvature, 0, length + 1)
        )
    )
    downward = courant * (
        window(low_edge, 1, length + 1)
        - 0.5
        * courant
        * (
            window(gradient, 1, length + 1)
            + (1.0 + courant * (2.0 / 3.0)) * window(curvature, 1, length + 1)
        )
    )
    fluxes = jnp.where(courant >= 0.0, upward, downward)
    return window(centre, 1, length) - (window(fluxes, 1, length) - window(fluxes, 0, length))


def to_frame(blocks, flip_flags):
    first_flag = (flip_flags[:, 0] == 1)[:, None, None, None, None]
    second_flag = (flip_flags[:, 1] == 1)[:, None, None, None, None]
    turned = jnp.where(first_flag, blocks[:, ::-1], blocks)
    return jnp.where(second_flag, turned[:, :, ::-1], turned)


def mixing_matrix(weights):
    totals = jnp.sum(weights, axis=-1, keepdims=True)
    identity = jnp.eye(weights.shape[-1], dtype=jnp.float32)
    return 0.6 * identity + 0.4 * (weights / totals)


def swapped(value, axis, mask):
    pairs = [(source, source ^ mask) for source in range(lax.axis_size(axis))]
    return lax.ppermute(value, axis, pairs)


def tile_stride(tiles):
    return max(2, tiles // 8)


def by_halos(tracers, courant_first, courant_second, weights, frame_flip):
    stride = tile_stride(lax.axis_size("tile"))
    extent = tracers.shape[1]
    fields = to_frame(tracers, frame_flip)
    first_faces = courant_first[..., None]
    second_faces = courant_second[..., None]
    for substep in range(SUBSTEPS):
        for along, faces, steps in ((1, first_faces, stride), (2, second_faces, 1)):
            size = fields.shape[along]
            high_cells = lax.slice_in_dim(fields, size - 3, size, axis=along)
            low_cells = lax.slice_in_dim(fields, 0, 3, axis=along)
            high_face = lax.slice_in_dim(faces, size - 1, size, axis=along)
            from_low, low_face = passed_along((high_cells, high_face), "tile", steps)
            from_high = passed_along(low_cells, "tile", -steps)
            fields = ppm_update(
                jnp.concatenate([from_low, fields, from_high], axis=along),
                jnp.concatenate([low_face, faces], axis=along),
                along,
            )
    advected = to_frame(fields, frame_flip)
    mixing = mixing_matrix(weights)
    columns = lax.all_to_all(advected, "lev", split_axis=1, concat_axis=3, tiled=True)
    mixed = jnp.einsum("txykl,txylq->txykq", mixing, columns, precision=lax.Precision.HIGHEST)
    return lax.all_to_all(mixed, "lev", split_axis=3, concat_axis=1, tiled=True)


class Plan:
    def __init__(self, side, levels, tracers, tiles, layers):
        self.side, self.levels, self.tracers = side, levels, tracers
        self.tiles, self.layers = tiles, layers
        self.cells = side * side
        self.full = levels // tiles
        self.spare = levels - self.full * tiles
        self.fits = (
            tiles == SUBLANES
            and tracers == LANES
            and self.cells * 2 == LANES
            and side % layers == 0
            and self.spare > 0
            and self.full > 0
            and tiles % self.spare == 0
        )
        if not self.fits:
            return
        self.groups = tiles // self.spare
        self.width = tracers // self.groups
        self.part_rows = self.cells // self.groups
        self.kinds = self.full + 1
        self.tail_at = self.full * self.cells
        self.courant_at = self.tail_at + self.part_rows
        self.flip_at = self.courant_at + self.kinds
        self.rows = -(-(self.flip_at + 1) // SUBLANES) * SUBLANES
        self.own_cells = self.cells // layers
        self.back_tail = self.full * self.own_cells
        self.back_part = self.own_cells // self.groups
        self.back_rows = self.back_tail + self.back_part
        self.all_levels = levels * layers
        self.fits = (
            self.cells % self.groups == 0
            and self.own_cells % self.groups == 0
            and self.part_rows % SUBLANES == 0
            and self.side == SUBLANES
            and self.own_cells % side == 0
            and self.kinds < SUBLANES
            and self.back_rows % FEW == 0
        )


def lane_group(shape, width):
    return lax.broadcasted_iota(jnp.int32, shape, 1) // width


def pack_kernel(p, x_ref, first_ref, second_ref, flip_ref, *refs):
    chips = p.tiles // 2
    own_refs, other_ref = refs[:chips], refs[chips]
    spare_ref, courant_ref, flags_ref, faces_ref, rest_ref, sems = refs[chips + 1 :]
    me = lax.axis_index("tile")
    slots = []
    for s in range(chips):
        slots.append((lax.bitwise_xor(me, 2 * s), own_refs[s]))
        slots.append((lax.bitwise_xor(me, 2 * s + 1), other_ref.at[s]))
    copies = []

    def fetch(source, target):
        copy = pltpu.make_async_copy(source, target, sems.at[len(copies)])
        copy.start()
        copies.append(copy)

    for source, target in ((first_ref, courant_ref.at[0]), (second_ref, courant_ref.at[1])):
        fetch(source, target)
    fetch(flip_ref, flags_ref)
    for h in range(p.spare):
        fetch(x_ref.at[:, p.full * p.tiles + h], spare_ref.at[h])
    small = 3
    for d, slot in slots:
        for f in range(p.full):
            fetch(x_ref.at[:, p.full * d + f], slot.at[pl.ds(f * p.side, p.side)])
    filler = jnp.zeros((p.side, LANES), jnp.float32)
    group = lane_group((p.side, LANES), p.width)
    for copy in copies[small : small + p.spare]:
        copy.wait()
    tall = p.part_rows // p.side
    for h in range(p.spare):
        for g in range(p.groups):
            for r in range(tall):
                rows = None
                for m in range(p.groups):
                    part = spare_ref[h, m * tall + r]
                    shift = (m - g) * p.width % LANES
                    moved = pltpu.roll(part, shift, 1) if shift else part
                    rows = moved if rows is None else jnp.where(group == m, moved, rows)
                rest_ref[h * p.groups + g, r] = rows
    for copy in copies[:small]:
        copy.wait()
    for way in range(2):
        for i in range(p.side):
            at = way * p.cells + i * p.side
            faces_ref[at : at + p.side, :] = filler
            faces_ref[at : at + p.side, : p.levels] = courant_ref[way, i]
    faces = faces_ref[...].T
    lane = lax.broadcasted_iota(jnp.int32, (1, LANES), 1)
    flags = flags_ref[...].astype(jnp.float32)
    flips = jnp.where(
        lane < p.cells,
        jnp.broadcast_to(flags[:, 0:1], (1, LANES)),
        jnp.broadcast_to(flags[:, 1:2], (1, LANES)),
    )
    for d in range(p.tiles):
        level = p.full * d
        rest = p.full * p.tiles + d // p.groups
        rest_ref[d, tall] = filler
        rest_ref[d, tall, : p.full, :] = faces[level : level + p.full]
        rest_ref[d, tall, p.full : p.kinds, :] = faces[rest : rest + 1]
        rest_ref[d, tall, p.kinds : p.kinds + 1, :] = flips
    for d, slot in slots:
        for r in range(tall + 1):
            slot[p.full * p.side + r] = rest_ref[d, r]
    for copy in copies[small + p.spare :]:
        copy.wait()


def advect_kernel(p, stride, *refs):
    tiles, side, cells = p.tiles, p.side, p.cells
    shape = (tiles, LANES)
    parts = refs[: -6]
    out_ref, in_ref, q_ref, near_ref, far_ref, mid_ref = refs[-6:]
    out_ref = out_ref.reshape(tiles * p.layers * p.back_rows, LANES)
    me = lax.axis_index("tile")
    each = tiles // len(parts)
    for s, part in enumerate(parts):
        for e in range(each):
            tile = lax.bitwise_xor(me, s * each + e)
            in_ref[pl.ds(pl.multiple_of(tile * p.rows, SUBLANES), p.rows), :] = part[
                e * p.rows : (e + 1) * p.rows, :
            ]

    def row(at):
        return in_ref[pl.ds(at, tiles, stride=p.rows), :]

    flips = row(p.flip_at)
    first_flip = jnp.broadcast_to(flips[:, 0:1], shape) > 0.5
    second_flip = jnp.broadcast_to(flips[:, cells : cells + 1], shape) > 0.5

    def turned(get):
        for i in range(side // 2):
            for j in range(side // 2):
                i2, j2 = side - 1 - i, side - 1 - j
                ll, hl, lh, hh = get(i, j), get(i2, j), get(i, j2), get(i2, j2)
                a, b = jnp.where(first_flip, hl, ll), jnp.where(first_flip, ll, hl)
                c, d = jnp.where(first_flip, hh, lh), jnp.where(first_flip, lh, hh)
                yield i * side + j, jnp.where(second_flip, c, a)
                yield i2 * side + j, jnp.where(second_flip, d, b)
                yield i * side + j2, jnp.where(second_flip, a, c)
                yield i2 * side + j2, jnp.where(second_flip, b, d)

    for kind in range(p.kinds):
        if kind < p.full:
            get = lambda i, j: row(kind * cells + i * side + j)
        else:

            def get(i, j):
                m, r = divmod(i * side + j, p.part_rows)
                value = row(p.tail_at + r)
                return pltpu.roll(value, LANES - m * p.width, 1) if m else value

        for cell, value in turned(get):
            q_ref[kind * cells + cell] = value
        courant = row(p.courant_at + kind)
        for at in range(2 * cells):
            c = jnp.broadcast_to(courant[:, at : at + 1], shape)
            e = jnp.abs(c)
            u = 1.0 - e
            cu = c * u
            near_ref[kind * 2 * cells + at] = (cu * u) * (1.0 / 12.0)
            far_ref[kind * 2 * cells + at] = (cu * e) * (-1.0 / 12.0)
            mid_ref[kind * 2 * cells + at] = (c * e) * (3.0 - 2.0 * e)

    def sweep(at, faces_at, step, shift):
        cell = [at + step * i for i in range(side)]
        face = [faces_at + step * i for i in range(side)]
        q = [q_ref[cell[i]] for i in range(side)]
        up = lambda v: pltpu.roll(v, shift, 0)
        down = lambda v: pltpu.roll(v, tiles - shift, 0)
        ext = [up(q[side - 1])] + q + [down(q[0]), down(q[1])]
        edge = [
            7.0 * (ext[i + 1] + ext[i + 2]) - (ext[i] + ext[i + 3]) for i in range(side)
        ]
        edges = [up(edge[side - 1])] + edge + [down(edge[0])]
        flux = []
        for i in range(side):
            near = near_ref[face[i]]
            upwind = near >= 0.0
            far = jnp.where(upwind, edges[i], edges[i + 2])
            mid = jnp.where(upwind, ext[i + 1], ext[i + 2])
            flux.append(near * edge[i] + far_ref[face[i]] * far + mid_ref[face[i]] * mid)
        fluxes = [up(flux[side - 1])] + flux
        for i in range(side):
            q_ref[cell[i]] = q[i] - (fluxes[i + 1] - fluxes[i])

    def step(count, carry):
        kind = count // SUBSTEPS
        at = kind * cells
        faces_at = kind * 2 * cells
        for j in range(side):
            sweep(at + j, faces_at + j, side, stride)
        for i in range(side):
            sweep(at + i * side, faces_at + cells + i * side, 1, 1)
        return carry

    lax.fori_loop(0, p.kinds * SUBSTEPS, step, 0)

    pitch = p.layers * p.back_rows

    def send(cell_layer, at, value):
        out_ref[pl.ds(cell_layer * p.back_rows + at, tiles, stride=pitch), :] = value

    for kind in range(p.kinds):
        back = turned(lambda i, j: q_ref[kind * cells + i * side + j])
        if kind < p.full:
            for cell, value in back:
                layer, own = divmod(cell, p.own_cells)
                send(layer, kind * p.own_cells + own, value)
        else:
            for cell, value in back:
                q_ref[kind * cells + cell] = value
    group = lane_group(shape, p.width)
    for layer in range(p.layers):
        for r in range(p.back_part):
            rows = None
            for m in range(p.groups):
                value = q_ref[p.full * cells + layer * p.own_cells + m * p.back_part + r]
                moved = pltpu.roll(value, m * p.width, 1) if m else value
                rows = moved if rows is None else jnp.where(group == m, moved, rows)
            send(layer, p.back_tail + r, rows)


def mix_kernel(p, in_ref, weights_ref, *refs):
    out_refs, (x_ref, all_ref) = refs[: p.layers], refs[p.layers :]
    tiles = p.tiles
    in_ref = in_ref.reshape(tiles * p.layers * p.back_rows, LANES)
    shape = (tiles, LANES)
    pitch = p.layers * p.back_rows
    group = lane_group(shape, p.width)
    part = lax.broadcasted_iota(jnp.int32, shape, 0) % p.groups
    places = [(group == g) & (part == g) for g in range(p.groups)]

    def row(layer, at):
        return in_ref[pl.ds(layer * p.back_rows + at, tiles, stride=pitch), :]

    for r in range(p.back_part):
        turned = []
        for layer in range(p.layers):
            value = row(layer, p.back_tail + r)
            turned.append([value] + [pltpu.roll(value, s * p.width, 1) for s in range(1, p.groups)])
        for m in range(p.groups):
            own = m * p.back_part + r
            for layer in range(p.layers):
                base = layer * p.levels
                for f in range(p.full):
                    x_ref[own, pl.ds(base + f, tiles, stride=p.full), :] = row(
                        layer, f * p.own_cells + own
                    )
                tail = jnp.zeros(shape, jnp.float32)
                for g in range(p.groups):
                    tail = jnp.where(places[g], turned[layer][(g - m) % p.groups], tail)
                reach = 1
                while reach < p.groups:
                    tail = tail + pltpu.roll(tail, tiles - reach, 0)
                    reach *= 2
                for h in range(p.spare):
                    at = base + p.full * tiles + h
                    x_ref[own, at : at + 1, :] = tail[h * p.groups : h * p.groups + 1]
    for own in range(p.own_cells):
        x = x_ref[own]
        weights = weights_ref[own]
        scale = 0.4 / jnp.sum(weights, axis=-1, keepdims=True)
        x_high = x.astype(jnp.bfloat16)
        x_low = (x - x_high.astype(jnp.float32)).astype(jnp.bfloat16)
        w_high = weights.astype(jnp.bfloat16)
        w_low = (weights - w_high.astype(jnp.float32)).astype(jnp.bfloat16)
        dot = functools.partial(jnp.dot, preferred_element_type=jnp.float32)
        total = dot(w_high, x_high) + (dot(w_high, x_low) + dot(w_low, x_high))
        all_ref[pl.ds(own, p.all_levels, stride=p.own_cells), :] = 0.6 * x + scale * total
    me = lax.axis_index("lev")
    size = p.levels * p.own_cells
    for s in range(p.layers):
        layer = lax.rem(me + s, p.layers)
        out_refs[s][...] = all_ref[pl.ds(pl.multiple_of(layer * size, SUBLANES), size), :]


def place_kernel(p, *refs):
    in_refs, out_ref = refs[: p.layers], refs[p.layers]
    me = lax.axis_index("lev")
    tall = p.own_cells // p.side
    for s in range(p.layers):
        layer = lax.rem(me - s + p.layers, p.layers)
        for level in range(p.levels):
            for r in range(tall):
                at = level * p.own_cells + r * p.side
                out_ref[layer * tall + r, level] = in_refs[s][at : at + p.side, :]


def in_vmem(count):
    return [pl.BlockSpec(memory_space=pltpu.VMEM)] * count


def params():
    return pltpu.CompilerParams(vmem_limit_bytes=VMEM_LIMIT)


def by_levels(p, tracers, courant_first, courant_second, weights, frame_flip):
    f32 = jnp.float32
    across = (p.side, p.levels, p.side, p.tracers)
    chips = p.tiles // 2
    blocks = (p.rows // p.side, p.side, LANES)
    *own, other = pl.pallas_call(
        functools.partial(pack_kernel, p),
        out_shape=[jax.ShapeDtypeStruct(blocks, f32)] * chips
        + [jax.ShapeDtypeStruct((chips,) + blocks, f32)],
        in_specs=[pl.BlockSpec(memory_space=pltpu.HBM)] * 4,
        out_specs=in_vmem(chips + 1),
        scratch_shapes=[
            pltpu.VMEM((p.spare, p.side, p.side, LANES), f32),
            pltpu.VMEM((2, p.side, p.side, p.levels), f32),
            pltpu.VMEM((1, 2), jnp.int32),
            pltpu.VMEM((LANES, LANES), f32),
            pltpu.VMEM((p.tiles, p.part_rows // p.side + 1, p.side, LANES), f32),
            pltpu.SemaphoreType.DMA((3 + p.tiles * p.full + p.spare,)),
        ],
        compiler_params=params(),
        name="pack",
    )(
        *(
            pltpu.with_memory_space_constraint(value, pltpu.HBM)
            for value in (
                tracers[0].transpose(0, 2, 1, 3),
                courant_first[0],
                courant_second[0],
                frame_flip,
            )
        )
    )
    got = swapped(other, "tile", 1)
    pieces = [None] * p.tiles
    for s in range(chips - 1, -1, -1):
        for e, block in ((0, own[s]), (1, got[s])):
            block = block.reshape(p.rows, LANES)
            pieces[2 * s + e] = swapped(block, "tile", 2 * s) if s else block
    moved = pl.pallas_call(
        functools.partial(advect_kernel, p, tile_stride(p.tiles)),
        out_shape=jax.ShapeDtypeStruct(
            (p.tiles * p.layers, p.back_rows // FEW, FEW, LANES), f32
        ),
        in_specs=in_vmem(len(pieces)),
        out_specs=pl.BlockSpec(memory_space=pltpu.VMEM),
        scratch_shapes=[
            pltpu.VMEM((p.tiles * p.rows, LANES), f32),
            pltpu.VMEM((p.kinds * p.cells, p.tiles, LANES), f32),
        ]
        + [pltpu.VMEM((p.kinds * 2 * p.cells, p.tiles, LANES), f32)] * 3,
        compiler_params=params(),
        name="advect",
    )(*pieces)
    columns = lax.all_to_all(
        moved,
        ("tile", "lev"),
        split_axis=0,
        concat_axis=0,
        tiled=True,
    )
    size = p.levels * p.own_cells
    mixed = pl.pallas_call(
        functools.partial(mix_kernel, p),
        out_shape=[jax.ShapeDtypeStruct((size, LANES), f32)] * p.layers,
        in_specs=in_vmem(2),
        out_specs=in_vmem(p.layers),
        scratch_shapes=[
            pltpu.VMEM((p.own_cells, p.all_levels, LANES), f32),
            pltpu.VMEM((p.all_levels * p.own_cells, LANES), f32),
        ],
        compiler_params=params(),
        name="mix",
    )(
        columns,
        weights.reshape(p.own_cells, p.all_levels, p.all_levels),
    )
    pieces = [mixed[0]] + [passed_along(mixed[s], "lev", s) for s in range(1, p.layers)]
    placed = pl.pallas_call(
        functools.partial(place_kernel, p),
        out_shape=jax.ShapeDtypeStruct(across, f32),
        in_specs=in_vmem(p.layers),
        out_specs=pl.BlockSpec(memory_space=pltpu.VMEM),
        compiler_params=params(),
        name="place",
    )(*pieces)
    return placed.transpose(0, 2, 1, 3)[None]


def on_device(tracers, courant_first, courant_second, weights, frame_flip):
    plan = Plan(
        tracers.shape[1],
        tracers.shape[3],
        tracers.shape[4],
        lax.axis_size("tile"),
        lax.axis_size("lev"),
    )
    if tracers.shape[1] == tracers.shape[2] and tracers.shape[0] == 1 and plan.fits:
        return by_levels(plan, tracers, courant_first, courant_second, weights, frame_flip)
    return by_halos(tracers, courant_first, courant_second, weights, frame_flip)


def solution(mesh):
    in_specs = (
        P("tile", None, None, "lev", None),
        P("tile", None, None, "lev"),
        P("tile", None, None, "lev"),
        P("tile", "lev", None, None, None),
        P("tile", None),
    )
    out_specs = P("tile", None, None, "lev", None)
    return jax.shard_map(
        on_device, mesh=mesh, in_specs=in_specs, out_specs=out_specs, check_vma=False
    )
```

```python
import functools

import jax
import jax.numpy as jnp
from jax import lax
from jax.experimental import pallas as pl
from jax.experimental.pallas import tpu as pltpu
from jax.sharding import PartitionSpec as P

SUBSTEPS = 3
SUBLANES = 8
LANES = 128
FEW = 4
VMEM_LIMIT = 40 * 1024 * 1024


def passed_along(value, axis, steps):
    count = lax.axis_size(axis)
    pairs = [(source, (source + steps) % count) for source in range(count)]
    return lax.ppermute(value, axis, pairs)


def ppm_update(extended, courant, along):
    length = extended.shape[along] - 6

    def window(values, offset, amount):
        return lax.slice_in_dim(values, offset, offset + amount, axis=along)

    interfaces = (
        7.0 * (window(extended, 1, length + 3) + window(extended, 2, length + 3))
        - (window(extended, 0, length + 3) + window(extended, 3, length + 3))
    ) / 12.0
    low_edge = window(interfaces, 0, length + 2)
    high_edge = window(interfaces, 1, length + 2)
    centre = window(extended, 2, length + 2)
    gradient = high_edge - low_edge
    curvature = 6.0 * centre - 3.0 * (low_edge + high_edge)
    upward = courant * (
        window(high_edge, 0, length + 1)
        - 0.5
        * courant
        * (
            window(gradient, 0, length + 1)
            - (1.0 - courant * (2.0 / 3.0)) * window(curvature, 0, length + 1)
        )
    )
    downward = courant * (
        window(low_edge, 1, length + 1)
        - 0.5
        * courant
        * (
            window(gradient, 1, length + 1)
            + (1.0 + courant * (2.0 / 3.0)) * window(curvature, 1, length + 1)
        )
    )
    fluxes = jnp.where(courant >= 0.0, upward, downward)
    return window(centre, 1, length) - (window(fluxes, 1, length) - window(fluxes, 0, length))


def to_frame(blocks, flip_flags):
    first_flag = (flip_flags[:, 0] == 1)[:, None, None, None, None]
    second_flag = (flip_flags[:, 1] == 1)[:, None, None, None, None]
    turned = jnp.where(first_flag, blocks[:, ::-1], blocks)
    return jnp.where(second_flag, turned[:, :, ::-1], turned)


def mixing_matrix(weights):
    totals = jnp.sum(weights, axis=-1, keepdims=True)
    identity = jnp.eye(weights.shape[-1], dtype=jnp.float32)
    return 0.6 * identity + 0.4 * (weights / totals)


def swapped(value, axis, mask):
    pairs = [(source, source ^ mask) for source in range(lax.axis_size(axis))]
    return lax.ppermute(value, axis, pairs)


def tile_stride(tiles):
    return max(2, tiles // 8)


def by_halos(tracers, courant_first, courant_second, weights, frame_flip):
    stride = tile_stride(lax.axis_size("tile"))
    extent = tracers.shape[1]
    fields = to_frame(tracers, frame_flip)
    first_faces = courant_first[..., None]
    second_faces = courant_second[..., None]
    for substep in range(SUBSTEPS):
        for along, faces, steps in ((1, first_faces, stride), (2, second_faces, 1)):
            size = fields.shape[along]
            high_cells = lax.slice_in_dim(fields, size - 3, size, axis=along)
            low_cells = lax.slice_in_dim(fields, 0, 3, axis=along)
            high_face = lax.slice_in_dim(faces, size - 1, size, axis=along)
            from_low, low_face = passed_along((high_cells, high_face), "tile", steps)
            from_high = passed_along(low_cells, "tile", -steps)
            fields = ppm_update(
                jnp.concatenate([from_low, fields, from_high], axis=along),
                jnp.concatenate([low_face, faces], axis=along),
                along,
            )
    advected = to_frame(fields, frame_flip)
    mixing = mixing_matrix(weights)
    columns = lax.all_to_all(advected, "lev", split_axis=1, concat_axis=3, tiled=True)
    mixed = jnp.einsum("txykl,txylq->txykq", mixing, columns, precision=lax.Precision.HIGHEST)
    return lax.all_to_all(mixed, "lev", split_axis=3, concat_axis=1, tiled=True)


class Plan:
    def __init__(self, side, levels, tracers, tiles, layers):
        self.side, self.levels, self.tracers = side, levels, tracers
        self.tiles, self.layers = tiles, layers
        self.cells = side * side
        self.full = levels // tiles
        self.spare = levels - self.full * tiles
        self.fits = (
            tiles == SUBLANES
            and tracers == LANES
            and self.cells * 2 == LANES
            and side % layers == 0
            and self.spare > 0
            and self.full > 0
            and tiles % self.spare == 0
        )
        if not self.fits:
            return
        self.groups = tiles // self.spare
        self.width = tracers // self.groups
        self.part_rows = self.cells // self.groups
        self.kinds = self.full + 1
        self.tail_at = self.full * self.cells
        self.courant_at = self.tail_at + self.part_rows
        self.flip_at = self.courant_at + self.kinds
        self.rows = -(-(self.flip_at + 1) // SUBLANES) * SUBLANES
        self.own_cells = self.cells // layers
        self.back_tail = self.full * self.own_cells
        self.back_part = self.own_cells // self.groups
        self.back_rows = self.back_tail + self.back_part
        self.all_levels = levels * layers
        self.fits = (
            self.cells % self.groups == 0
            and self.own_cells % self.groups == 0
            and self.part_rows % (2 * side) == 0
            and self.side == SUBLANES
            and self.own_cells % side == 0
            and self.kinds < SUBLANES
            and self.back_rows % FEW == 0
        )


def lane_group(shape, width):
    return lax.broadcasted_iota(jnp.int32, shape, 1) // width


def pack_kernel(p, x_ref, first_ref, second_ref, flip_ref, *refs):
    chips = p.tiles // 2
    own_refs, other_ref = refs[:chips], refs[chips]
    spare_ref, courant_ref, flags_ref, faces_ref, rest_ref, sems = refs[chips + 1 :]
    me = lax.axis_index("tile")
    slots = []
    for s in range(chips):
        slots.append((lax.bitwise_xor(me, 2 * s), own_refs[s]))
        slots.append((lax.bitwise_xor(me, 2 * s + 1), other_ref.at[s]))
    copies = []

    def fetch(source, target):
        copy = pltpu.make_async_copy(source, target, sems.at[len(copies)])
        copy.start()
        copies.append(copy)

    for source, target in ((first_ref, courant_ref.at[0]), (second_ref, courant_ref.at[1])):
        fetch(source, target)
    fetch(flip_ref, flags_ref)
    fetch(x_ref.at[:, pl.ds(p.full * p.tiles, p.spare)], spare_ref)
    small = 3
    for d, slot in slots:
        fetch(
            x_ref.at[:, pl.ds(p.full * d, p.full)],
            slot.at[pl.ds(0, p.full * p.side)].reshape(p.side, p.full, p.side, LANES),
        )
    filler = jnp.zeros((p.side, LANES), jnp.float32)
    group = lane_group((p.side, LANES), p.width)
    copies[small].wait()
    tall = p.part_rows // p.side
    for h in range(p.spare):
        for g in range(p.groups):
            for r in range(tall):
                rows = None
                for m in range(p.groups):
                    part = spare_ref[m * tall + r, h]
                    shift = (m - g) * p.width % LANES
                    moved = pltpu.roll(part, shift, 1) if shift else part
                    rows = moved if rows is None else jnp.where(group == m, moved, rows)
                rest_ref[h * p.groups + g, r] = rows
    for copy in copies[:small]:
        copy.wait()
    for way in range(2):
        for i in range(p.side):
            at = way * p.cells + i * p.side
            faces_ref[at : at + p.side, :] = filler
            faces_ref[at : at + p.side, : p.levels] = courant_ref[way, i]
    faces = faces_ref[...].T
    lane = lax.broadcasted_iota(jnp.int32, (1, LANES), 1)
    flags = flags_ref[...].astype(jnp.float32)
    flips = jnp.where(
        lane < p.cells,
        jnp.broadcast_to(flags[:, 0:1], (1, LANES)),
        jnp.broadcast_to(flags[:, 1:2], (1, LANES)),
    )
    for d in range(p.tiles):
        level = p.full * d
        rest = p.full * p.tiles + d // p.groups
        rest_ref[d, tall] = filler
        rest_ref[d, tall, : p.full, :] = faces[level : level + p.full]
        rest_ref[d, tall, p.full : p.kinds, :] = faces[rest : rest + 1]
        rest_ref[d, tall, p.kinds : p.kinds + 1, :] = flips
    for d, slot in slots:
        for r in range(tall + 1):
            slot[p.full * p.side + r] = rest_ref[d, r]
    for copy in copies[small + 1 :]:
        copy.wait()


def advect_kernel(p, stride, *refs):
    tiles, side, cells = p.tiles, p.side, p.cells
    shape = (tiles, LANES)
    parts = refs[: -6]
    out_ref, in_ref, q_ref, near_ref, far_ref, mid_ref = refs[-6:]
    out_ref = out_ref.reshape(tiles * p.layers * p.back_rows, LANES)
    me = lax.axis_index("tile")
    each = tiles // len(parts)
    for s, part in enumerate(parts):
        for e in range(each):
            tile = lax.bitwise_xor(me, s * each + e)
            in_ref[pl.ds(pl.multiple_of(tile * p.rows, SUBLANES), p.rows), :] = part[
                e * p.rows : (e + 1) * p.rows, :
            ]

    def row(at):
        return in_ref[pl.ds(at, tiles, stride=p.rows), :]

    flips = row(p.flip_at)
    first_flip = jnp.broadcast_to(flips[:, 0:1], shape) > 0.5
    second_flip = jnp.broadcast_to(flips[:, cells : cells + 1], shape) > 0.5
    group = lane_group(shape, p.width)
    tall = p.part_rows // side

    def reversed_groups(value):
        turned = {}
        result = None
        for g in range(p.groups):
            by = (2 * g + 1) % p.groups
            if by not in turned:
                turned[by] = pltpu.roll(value, by * p.width, 1) if by else value
            result = turned[by] if result is None else jnp.where(group == g, turned[by], result)
        return result

    def mirrored(get, height, back):
        for i in range(height // 2):
            for j in range(side // 2):
                i2, j2 = height - 1 - i, side - 1 - j
                ll, hl, lh, hh = get(i, j), get(i2, j), get(i, j2), get(i2, j2)
                a, b = jnp.where(first_flip, back(hl), ll), jnp.where(first_flip, back(ll), hl)
                c, d = jnp.where(first_flip, back(hh), lh), jnp.where(first_flip, back(lh), hh)
                yield i * side + j, jnp.where(second_flip, c, a)
                yield i2 * side + j, jnp.where(second_flip, d, b)
                yield i * side + j2, jnp.where(second_flip, a, c)
                yield i2 * side + j2, jnp.where(second_flip, b, d)

    def plain(value):
        return value

    def set_faces(at, c):
        e = jnp.abs(c)
        u = 1.0 - e
        cu = c * u
        near_ref[at] = (cu * u) * (1.0 / 12.0)
        far_ref[at] = (cu * e) * (-1.0 / 12.0)
        mid_ref[at] = (c * e) * (3.0 - 2.0 * e)

    tail = p.full * cells
    tail_faces = p.full * 2 * cells
    for kind in range(p.full):
        for cell, value in mirrored(
            lambda i, j: row((i * p.full + kind) * side + j), side, plain
        ):
            q_ref[kind * cells + cell] = value
        courant = row(p.courant_at + kind)
        for at in range(2 * cells):
            set_faces(kind * 2 * cells + at, jnp.broadcast_to(courant[:, at : at + 1], shape))
    for cell, value in mirrored(
        lambda i, j: row(p.tail_at + i * side + j), tall, reversed_groups
    ):
        q_ref[tail + cell] = value
    courant = row(p.courant_at + p.full)
    for way in range(2):
        for r in range(p.part_rows):
            c = None
            for m in range(p.groups):
                at = way * cells + m * p.part_rows + r
                value = jnp.broadcast_to(courant[:, at : at + 1], shape)
                c = value if c is None else jnp.where(group == m, value, c)
            set_faces(tail_faces + way * p.part_rows + r, c)

    def sweep(at, faces_at, step, length, up, down):
        cell = [at + step * i for i in range(length)]
        face = [faces_at + step * i for i in range(length)]
        q = [q_ref[cell[i]] for i in range(length)]
        ext = [up(q[length - 1])] + q + [down(q[0]), down(q[1])]
        edge = [
            7.0 * (ext[i + 1] + ext[i + 2]) - (ext[i] + ext[i + 3]) for i in range(length)
        ]
        edges = [up(edge[length - 1])] + edge + [down(edge[0])]
        flux = []
        for i in range(length):
            near = near_ref[face[i]]
            upwind = near >= 0.0
            far = jnp.where(upwind, edges[i], edges[i + 2])
            mid = jnp.where(upwind, ext[i + 1], ext[i + 2])
            flux.append(near * edge[i] + far_ref[face[i]] * far + mid_ref[face[i]] * mid)
        fluxes = [up(flux[length - 1])] + flux
        for i in range(length):
            q_ref[cell[i]] = q[i] - (fluxes[i + 1] - fluxes[i])

    def low_tile(shift):
        return lambda v: pltpu.roll(v, shift, 0)

    def high_tile(shift):
        return lambda v: pltpu.roll(v, tiles - shift, 0)

    def low_group(v):
        moved = pltpu.roll(v, p.width, 1)
        return jnp.where(group == 0, low_tile(stride)(moved), moved)

    def high_group(v):
        moved = pltpu.roll(v, LANES - p.width, 1)
        return jnp.where(group == p.groups - 1, high_tile(stride)(moved), moved)

    def step(count, carry):
        for j in range(side):
            for kind in range(p.full):
                at, faces_at = kind * cells + j, kind * 2 * cells + j
                sweep(at, faces_at, side, side, low_tile(stride), high_tile(stride))
            sweep(tail + j, tail_faces + j, side, tall, low_group, high_group)
        for i in range(side):
            for kind in range(p.full):
                at, faces_at = kind * cells + i * side, (kind * 2 + 1) * cells + i * side
                sweep(at, faces_at, 1, side, low_tile(1), high_tile(1))
            if i < tall:
                at, faces_at = tail + i * side, tail_faces + p.part_rows + i * side
                sweep(at, faces_at, 1, side, low_tile(1), high_tile(1))
        return carry

    lax.fori_loop(0, SUBSTEPS, step, 0)

    pitch = p.layers * p.back_rows

    def send(layer, at, value):
        out_ref[pl.ds(layer * p.back_rows + at, tiles, stride=pitch), :] = value

    for kind in range(p.full):
        for cell, value in mirrored(
            lambda i, j: q_ref[kind * cells + i * side + j], side, plain
        ):
            layer, own = divmod(cell, p.own_cells)
            send(layer, kind * p.own_cells + own, value)
    rest = dict(mirrored(lambda i, j: q_ref[tail + i * side + j], tall, reversed_groups))
    for layer in range(p.layers):
        for r in range(p.back_part):
            rows = None
            for m in range(p.groups):
                at, source = divmod(
                    layer * p.own_cells + m * p.back_part + r, p.part_rows
                )[::-1]
                shift = (m - source) * p.width % LANES
                moved = pltpu.roll(rest[at], shift, 1) if shift else rest[at]
                rows = moved if rows is None else jnp.where(group == m, moved, rows)
            send(layer, p.back_tail + r, rows)


def mix_kernel(p, in_ref, weights_ref, *refs):
    out_refs, (x_ref, all_ref) = refs[: p.layers], refs[p.layers :]
    tiles = p.tiles
    in_ref = in_ref.reshape(tiles * p.layers * p.back_rows, LANES)
    shape = (tiles, LANES)
    pitch = p.layers * p.back_rows
    group = lane_group(shape, p.width)
    part = lax.broadcasted_iota(jnp.int32, shape, 0) % p.groups
    places = [(group == g) & (part == g) for g in range(p.groups)]

    def row(layer, at):
        return in_ref[pl.ds(layer * p.back_rows + at, tiles, stride=pitch), :]

    for r in range(p.back_part):
        turned = []
        for layer in range(p.layers):
            value = row(layer, p.back_tail + r)
            turned.append([value] + [pltpu.roll(value, s * p.width, 1) for s in range(1, p.groups)])
        for m in range(p.groups):
            own = m * p.back_part + r
            for layer in range(p.layers):
                base = layer * p.levels
                for f in range(p.full):
                    x_ref[own, pl.ds(base + f, tiles, stride=p.full), :] = row(
                        layer, f * p.own_cells + own
                    )
                tail = jnp.zeros(shape, jnp.float32)
                for g in range(p.groups):
                    tail = jnp.where(places[g], turned[layer][(g - m) % p.groups], tail)
                reach = 1
                while reach < p.groups:
                    tail = tail + pltpu.roll(tail, tiles - reach, 0)
                    reach *= 2
                for h in range(p.spare):
                    at = base + p.full * tiles + h
                    x_ref[own, at : at + 1, :] = tail[h * p.groups : h * p.groups + 1]
    for own in range(p.own_cells):
        x = x_ref[own]
        weights = weights_ref[own]
        scale = 0.4 / jnp.sum(weights, axis=-1, keepdims=True)
        x_high = x.astype(jnp.bfloat16)
        x_low = (x - x_high.astype(jnp.float32)).astype(jnp.bfloat16)
        w_high = weights.astype(jnp.bfloat16)
        w_low = (weights - w_high.astype(jnp.float32)).astype(jnp.bfloat16)
        dot = functools.partial(jnp.dot, preferred_element_type=jnp.float32)
        total = dot(w_high, x_high) + (dot(w_high, x_low) + dot(w_low, x_high))
        all_ref[pl.ds(own, p.all_levels, stride=p.own_cells), :] = 0.6 * x + scale * total
    me = lax.axis_index("lev")
    size = p.levels * p.own_cells
    for s in range(p.layers):
        layer = lax.rem(me + s, p.layers)
        out_refs[s][...] = all_ref[pl.ds(pl.multiple_of(layer * size, SUBLANES), size), :]


def place_kernel(p, order, *refs):
    in_refs, out_ref, sems = refs[: p.layers], refs[p.layers], refs[p.layers + 1]
    me = lax.axis_index("lev")
    tall = p.own_cells // p.side
    copies = []
    for n, s in enumerate(order):
        layer = lax.rem(me - s + p.layers, p.layers)
        piece = in_refs[n].reshape(p.levels, tall, p.side, LANES)
        for r in range(tall):
            copies.append(
                pltpu.make_async_copy(
                    piece.at[:, r], out_ref.at[layer * tall + r], sems.at[len(copies)]
                )
            )
            copies[-1].start()
    for copy in copies:
        copy.wait()


def in_vmem(count):
    return [pl.BlockSpec(memory_space=pltpu.VMEM)] * count


def params():
    return pltpu.CompilerParams(vmem_limit_bytes=VMEM_LIMIT)


def by_levels(p, tracers, courant_first, courant_second, weights, frame_flip):
    f32 = jnp.float32
    across = (p.side, p.levels, p.side, p.tracers)
    chips = p.tiles // 2
    blocks = (p.rows // p.side, p.side, LANES)
    *own, other = pl.pallas_call(
        functools.partial(pack_kernel, p),
        out_shape=[jax.ShapeDtypeStruct(blocks, f32)] * chips
        + [jax.ShapeDtypeStruct((chips,) + blocks, f32)],
        in_specs=[pl.BlockSpec(memory_space=pltpu.HBM)] * 4,
        out_specs=in_vmem(chips + 1),
        scratch_shapes=[
            pltpu.VMEM((p.side, p.spare, p.side, LANES), f32),
            pltpu.VMEM((2, p.side, p.side, p.levels), f32),
            pltpu.VMEM((1, 2), jnp.int32),
            pltpu.VMEM((LANES, LANES), f32),
            pltpu.VMEM((p.tiles, p.part_rows // p.side + 1, p.side, LANES), f32),
            pltpu.SemaphoreType.DMA((4 + p.tiles,)),
        ],
        compiler_params=params(),
        name="pack",
    )(
        *(
            pltpu.with_memory_space_constraint(value, pltpu.HBM)
            for value in (
                tracers[0].transpose(0, 2, 1, 3),
                courant_first[0],
                courant_second[0],
                frame_flip,
            )
        )
    )
    got = swapped(other, "tile", 1)
    pieces = [None] * p.tiles
    for s in range(chips - 1, -1, -1):
        for e, block in ((0, own[s]), (1, got[s])):
            block = block.reshape(p.rows, LANES)
            pieces[2 * s + e] = swapped(block, "tile", 2 * s) if s else block
    moved = pl.pallas_call(
        functools.partial(advect_kernel, p, tile_stride(p.tiles)),
        out_shape=jax.ShapeDtypeStruct(
            (p.tiles * p.layers, p.back_rows // FEW, FEW, LANES), f32
        ),
        in_specs=in_vmem(len(pieces)),
        out_specs=pl.BlockSpec(memory_space=pltpu.VMEM),
        scratch_shapes=[
            pltpu.VMEM((p.tiles * p.rows, LANES), f32),
            pltpu.VMEM((p.full * p.cells + p.part_rows, p.tiles, LANES), f32),
        ]
        + [pltpu.VMEM((2 * (p.full * p.cells + p.part_rows), p.tiles, LANES), f32)] * 3,
        compiler_params=params(),
        name="advect",
    )(*pieces)
    columns = lax.all_to_all(
        moved,
        ("tile", "lev"),
        split_axis=0,
        concat_axis=0,
        tiled=True,
    )
    size = p.levels * p.own_cells
    mixed = pl.pallas_call(
        functools.partial(mix_kernel, p),
        out_shape=[jax.ShapeDtypeStruct((size, LANES), f32)] * p.layers,
        in_specs=in_vmem(2),
        out_specs=in_vmem(p.layers),
        scratch_shapes=[
            pltpu.VMEM((p.own_cells, p.all_levels, LANES), f32),
            pltpu.VMEM((p.all_levels * p.own_cells, LANES), f32),
        ],
        compiler_params=params(),
        name="mix",
    )(
        columns,
        weights.reshape(p.own_cells, p.all_levels, p.all_levels),
    )
    pieces = [mixed[0]] + [passed_along(mixed[s], "lev", s) for s in range(1, p.layers)]
    order = sorted(range(p.layers), key=lambda s: -min(s, p.layers - s) if s else -p.layers)
    placed = pl.pallas_call(
        functools.partial(place_kernel, p, order),
        out_shape=jax.ShapeDtypeStruct(across, f32),
        in_specs=in_vmem(p.layers),
        out_specs=pl.BlockSpec(memory_space=pltpu.HBM),
        scratch_shapes=[pltpu.SemaphoreType.DMA((p.cells // p.side,))],
        compiler_params=params(),
        name="place",
    )(*(pieces[s] for s in order))
    return placed.transpose(0, 2, 1, 3)[None]


def on_device(tracers, courant_first, courant_second, weights, frame_flip):
    plan = Plan(
        tracers.shape[1],
        tracers.shape[3],
        tracers.shape[4],
        lax.axis_size("tile"),
        lax.axis_size("lev"),
    )
    if tracers.shape[1] == tracers.shape[2] and tracers.shape[0] == 1 and plan.fits:
        return by_levels(plan, tracers, courant_first, courant_second, weights, frame_flip)
    return by_halos(tracers, courant_first, courant_second, weights, frame_flip)


def solution(mesh):
    in_specs = (
        P("tile", None, None, "lev", None),
        P("tile", None, None, "lev"),
        P("tile", None, None, "lev"),
        P("tile", "lev", None, None, None),
        P("tile", None),
    )
    out_specs = P("tile", None, None, "lev", None)
    return jax.shard_map(
        on_device, mesh=mesh, in_specs=in_specs, out_specs=out_specs, check_vma=False
    )
```

```python
import functools

import jax
import jax.numpy as jnp
from jax import lax
from jax.experimental import pallas as pl
from jax.experimental.pallas import tpu as pltpu
from jax.sharding import PartitionSpec as P

SUBSTEPS = 3
SUBLANES = 8
LANES = 128
FEW = 4
VMEM_LIMIT = 40 * 1024 * 1024


def passed_along(value, axis, steps):
    count = lax.axis_size(axis)
    pairs = [(source, (source + steps) % count) for source in range(count)]
    return lax.ppermute(value, axis, pairs)


def ppm_update(extended, courant, along):
    length = extended.shape[along] - 6

    def window(values, offset, amount):
        return lax.slice_in_dim(values, offset, offset + amount, axis=along)

    interfaces = (
        7.0 * (window(extended, 1, length + 3) + window(extended, 2, length + 3))
        - (window(extended, 0, length + 3) + window(extended, 3, length + 3))
    ) / 12.0
    low_edge = window(interfaces, 0, length + 2)
    high_edge = window(interfaces, 1, length + 2)
    centre = window(extended, 2, length + 2)
    gradient = high_edge - low_edge
    curvature = 6.0 * centre - 3.0 * (low_edge + high_edge)
    upward = courant * (
        window(high_edge, 0, length + 1)
        - 0.5
        * courant
        * (
            window(gradient, 0, length + 1)
            - (1.0 - courant * (2.0 / 3.0)) * window(curvature, 0, length + 1)
        )
    )
    downward = courant * (
        window(low_edge, 1, length + 1)
        - 0.5
        * courant
        * (
            window(gradient, 1, length + 1)
            + (1.0 + courant * (2.0 / 3.0)) * window(curvature, 1, length + 1)
        )
    )
    fluxes = jnp.where(courant >= 0.0, upward, downward)
    return window(centre, 1, length) - (window(fluxes, 1, length) - window(fluxes, 0, length))


def to_frame(blocks, flip_flags):
    first_flag = (flip_flags[:, 0] == 1)[:, None, None, None, None]
    second_flag = (flip_flags[:, 1] == 1)[:, None, None, None, None]
    turned = jnp.where(first_flag, blocks[:, ::-1], blocks)
    return jnp.where(second_flag, turned[:, :, ::-1], turned)


def mixing_matrix(weights):
    totals = jnp.sum(weights, axis=-1, keepdims=True)
    identity = jnp.eye(weights.shape[-1], dtype=jnp.float32)
    return 0.6 * identity + 0.4 * (weights / totals)


def swapped(value, axis, mask):
    pairs = [(source, source ^ mask) for source in range(lax.axis_size(axis))]
    return lax.ppermute(value, axis, pairs)


def tile_stride(tiles):
    return max(2, tiles // 8)


def by_halos(tracers, courant_first, courant_second, weights, frame_flip):
    stride = tile_stride(lax.axis_size("tile"))
    extent = tracers.shape[1]
    fields = to_frame(tracers, frame_flip)
    first_faces = courant_first[..., None]
    second_faces = courant_second[..., None]
    for substep in range(SUBSTEPS):
        for along, faces, steps in ((1, first_faces, stride), (2, second_faces, 1)):
            size = fields.shape[along]
            high_cells = lax.slice_in_dim(fields, size - 3, size, axis=along)
            low_cells = lax.slice_in_dim(fields, 0, 3, axis=along)
            high_face = lax.slice_in_dim(faces, size - 1, size, axis=along)
            from_low, low_face = passed_along((high_cells, high_face), "tile", steps)
            from_high = passed_along(low_cells, "tile", -steps)
            fields = ppm_update(
                jnp.concatenate([from_low, fields, from_high], axis=along),
                jnp.concatenate([low_face, faces], axis=along),
                along,
            )
    advected = to_frame(fields, frame_flip)
    mixing = mixing_matrix(weights)
    columns = lax.all_to_all(advected, "lev", split_axis=1, concat_axis=3, tiled=True)
    mixed = jnp.einsum("txykl,txylq->txykq", mixing, columns, precision=lax.Precision.HIGHEST)
    return lax.all_to_all(mixed, "lev", split_axis=3, concat_axis=1, tiled=True)


class Plan:
    def __init__(self, side, levels, tracers, tiles, layers):
        self.side, self.levels, self.tracers = side, levels, tracers
        self.tiles, self.layers = tiles, layers
        self.cells = side * side
        self.full = levels // tiles
        self.spare = levels - self.full * tiles
        self.fits = (
            tiles == SUBLANES
            and tracers == LANES
            and self.cells * 2 == LANES
            and side % layers == 0
            and self.spare > 0
            and self.full > 0
            and tiles % self.spare == 0
        )
        if not self.fits:
            return
        self.groups = tiles // self.spare
        self.width = tracers // self.groups
        self.part_rows = self.cells // self.groups
        self.kinds = self.full + 1
        self.tail_at = self.full * self.cells
        self.courant_at = self.tail_at + self.part_rows
        self.flip_at = self.courant_at + self.kinds
        self.rows = -(-(self.flip_at + 1) // SUBLANES) * SUBLANES
        self.own_cells = self.cells // layers
        self.back_tail = self.full * self.own_cells
        self.back_part = self.own_cells // self.groups
        self.back_rows = self.back_tail + self.back_part
        self.all_levels = levels * layers
        self.fits = (
            self.cells % self.groups == 0
            and self.own_cells % self.groups == 0
            and self.part_rows % (2 * side) == 0
            and self.side == SUBLANES
            and self.own_cells % side == 0
            and self.kinds < SUBLANES
            and self.back_rows % FEW == 0
        )


def lane_group(shape, width):
    return lax.broadcasted_iota(jnp.int32, shape, 1) // width


def pack_kernel(p, x_ref, first_ref, second_ref, flip_ref, *refs):
    chips = p.tiles // 2
    own_refs, other_ref = refs[:chips], refs[chips]
    spare_ref, courant_ref, flags_ref, faces_ref, rest_ref, sems = refs[chips + 1 :]
    me = lax.axis_index("tile")
    slots = []
    for s in range(chips):
        slots.append((lax.bitwise_xor(me, 2 * s), own_refs[s]))
        slots.append((lax.bitwise_xor(me, 2 * s + 1), other_ref.at[s]))
    copies = []

    def fetch(source, target):
        copy = pltpu.make_async_copy(source, target, sems.at[len(copies)])
        copy.start()
        copies.append(copy)

    for source, target in ((first_ref, courant_ref.at[0]), (second_ref, courant_ref.at[1])):
        fetch(source, target)
    fetch(flip_ref, flags_ref)
    fetch(x_ref.at[:, pl.ds(p.full * p.tiles, p.spare)], spare_ref)
    small = 3
    for d, slot in slots:
        fetch(
            x_ref.at[:, pl.ds(p.full * d, p.full)],
            slot.at[pl.ds(0, p.full * p.side)].reshape(p.side, p.full, p.side, LANES),
        )
    filler = jnp.zeros((p.side, LANES), jnp.float32)
    group = lane_group((p.side, LANES), p.width)
    copies[small].wait()
    tall = p.part_rows // p.side
    for h in range(p.spare):
        for g in range(p.groups):
            for r in range(tall):
                rows = None
                for m in range(p.groups):
                    part = spare_ref[m * tall + r, h]
                    shift = (m - g) * p.width % LANES
                    moved = pltpu.roll(part, shift, 1) if shift else part
                    rows = moved if rows is None else jnp.where(group == m, moved, rows)
                rest_ref[h * p.groups + g, r] = rows
    for copy in copies[:small]:
        copy.wait()
    for way in range(2):
        for i in range(p.side):
            at = way * p.cells + i * p.side
            faces_ref[at : at + p.side, :] = filler
            faces_ref[at : at + p.side, : p.levels] = courant_ref[way, i]
    faces = faces_ref[...].T
    lane = lax.broadcasted_iota(jnp.int32, (1, LANES), 1)
    flags = flags_ref[...].astype(jnp.float32)
    flips = jnp.where(
        lane < p.cells,
        jnp.broadcast_to(flags[:, 0:1], (1, LANES)),
        jnp.broadcast_to(flags[:, 1:2], (1, LANES)),
    )
    for d in range(p.tiles):
        level = p.full * d
        rest = p.full * p.tiles + d // p.groups
        rest_ref[d, tall] = filler
        rest_ref[d, tall, : p.full, :] = faces[level : level + p.full]
        rest_ref[d, tall, p.full : p.kinds, :] = faces[rest : rest + 1]
        rest_ref[d, tall, p.kinds : p.kinds + 1, :] = flips
    for d, slot in slots:
        for r in range(tall + 1):
            slot[p.full * p.side + r] = rest_ref[d, r]
    for copy in copies[small + 1 :]:
        copy.wait()


def advect_kernel(p, stride, *refs):
    tiles, side, cells = p.tiles, p.side, p.cells
    shape = (tiles, LANES)
    parts = refs[: -6]
    out_ref, in_ref, q_ref, near_ref, far_ref, mid_ref = refs[-6:]
    out_ref = out_ref.reshape(tiles * p.layers * p.back_rows, LANES)
    me = lax.axis_index("tile")
    each = tiles // len(parts)
    for s, part in enumerate(parts):
        for e in range(each):
            tile = lax.bitwise_xor(me, s * each + e)
            in_ref[pl.ds(pl.multiple_of(tile * p.rows, SUBLANES), p.rows), :] = part[
                e * p.rows : (e + 1) * p.rows, :
            ]

    def row(at):
        return in_ref[pl.ds(at, tiles, stride=p.rows), :]

    flips = row(p.flip_at)
    first_flip = jnp.broadcast_to(flips[:, 0:1], shape) > 0.5
    second_flip = jnp.broadcast_to(flips[:, cells : cells + 1], shape) > 0.5
    group = lane_group(shape, p.width)
    tall = p.part_rows // side

    def reversed_groups(value):
        turned = {}
        result = None
        for g in range(p.groups):
            by = (2 * g + 1) % p.groups
            if by not in turned:
                turned[by] = pltpu.roll(value, by * p.width, 1) if by else value
            result = turned[by] if result is None else jnp.where(group == g, turned[by], result)
        return result

    def mirrored(get, height, back):
        for i in range(height // 2):
            for j in range(side // 2):
                i2, j2 = height - 1 - i, side - 1 - j
                ll, hl, lh, hh = get(i, j), get(i2, j), get(i, j2), get(i2, j2)
                a, b = jnp.where(first_flip, back(hl), ll), jnp.where(first_flip, back(ll), hl)
                c, d = jnp.where(first_flip, back(hh), lh), jnp.where(first_flip, back(lh), hh)
                yield i * side + j, jnp.where(second_flip, c, a)
                yield i2 * side + j, jnp.where(second_flip, d, b)
                yield i * side + j2, jnp.where(second_flip, a, c)
                yield i2 * side + j2, jnp.where(second_flip, b, d)

    def plain(value):
        return value

    def set_faces(at, c):
        e = jnp.abs(c)
        u = 1.0 - e
        cu = c * u
        near_ref[at] = (cu * u) * (1.0 / 12.0)
        far_ref[at] = (cu * e) * (-1.0 / 12.0)
        mid_ref[at] = (c * e) * (3.0 - 2.0 * e)

    tail = p.full * cells
    tail_faces = p.full * 2 * cells
    for kind in range(p.full):
        for cell, value in mirrored(
            lambda i, j: row((i * p.full + kind) * side + j), side, plain
        ):
            q_ref[kind * cells + cell] = value
        courant = row(p.courant_at + kind)
        for at in range(2 * cells):
            set_faces(kind * 2 * cells + at, jnp.broadcast_to(courant[:, at : at + 1], shape))
    for cell, value in mirrored(
        lambda i, j: row(p.tail_at + i * side + j), tall, reversed_groups
    ):
        q_ref[tail + cell] = value
    courant = row(p.courant_at + p.full)
    for way in range(2):
        for r in range(p.part_rows):
            c = None
            for m in range(p.groups):
                at = way * cells + m * p.part_rows + r
                value = jnp.broadcast_to(courant[:, at : at + 1], shape)
                c = value if c is None else jnp.where(group == m, value, c)
            set_faces(tail_faces + way * p.part_rows + r, c)

    def sweep(at, faces_at, step, length, up, down):
        cell = [at + step * i for i in range(length)]
        face = [faces_at + step * i for i in range(length)]
        q = [q_ref[cell[i]] for i in range(length)]
        ext = [up(q[length - 1])] + q + [down(q[0]), down(q[1])]
        edge = [
            7.0 * (ext[i + 1] + ext[i + 2]) - (ext[i] + ext[i + 3]) for i in range(length)
        ]
        edges = [up(edge[length - 1])] + edge + [down(edge[0])]
        flux = []
        for i in range(length):
            near = near_ref[face[i]]
            upwind = near >= 0.0
            far = jnp.where(upwind, edges[i], edges[i + 2])
            mid = jnp.where(upwind, ext[i + 1], ext[i + 2])
            flux.append(near * edge[i] + far_ref[face[i]] * far + mid_ref[face[i]] * mid)
        fluxes = [up(flux[length - 1])] + flux
        for i in range(length):
            q_ref[cell[i]] = q[i] - (fluxes[i + 1] - fluxes[i])

    def low_tile(shift):
        return lambda v: pltpu.roll(v, shift, 0)

    def high_tile(shift):
        return lambda v: pltpu.roll(v, tiles - shift, 0)

    def low_group(v):
        moved = pltpu.roll(v, p.width, 1)
        return jnp.where(group == 0, low_tile(stride)(moved), moved)

    def high_group(v):
        moved = pltpu.roll(v, LANES - p.width, 1)
        return jnp.where(group == p.groups - 1, high_tile(stride)(moved), moved)

    def step(count, carry):
        for j in range(side):
            for kind in range(p.full):
                at, faces_at = kind * cells + j, kind * 2 * cells + j
                sweep(at, faces_at, side, side, low_tile(stride), high_tile(stride))
            sweep(tail + j, tail_faces + j, side, tall, low_group, high_group)
        for i in range(side):
            for kind in range(p.full):
                at, faces_at = kind * cells + i * side, (kind * 2 + 1) * cells + i * side
                sweep(at, faces_at, 1, side, low_tile(1), high_tile(1))
            if i < tall:
                at, faces_at = tail + i * side, tail_faces + p.part_rows + i * side
                sweep(at, faces_at, 1, side, low_tile(1), high_tile(1))
        return carry

    lax.fori_loop(0, SUBSTEPS, step, 0)

    pitch = p.layers * p.back_rows

    def send(layer, at, value):
        out_ref[pl.ds(layer * p.back_rows + at, tiles, stride=pitch), :] = value

    for kind in range(p.full):
        for cell, value in mirrored(
            lambda i, j: q_ref[kind * cells + i * side + j], side, plain
        ):
            layer, own = divmod(cell, p.own_cells)
            send(layer, kind * p.own_cells + own, value)
    rest = dict(mirrored(lambda i, j: q_ref[tail + i * side + j], tall, reversed_groups))
    for layer in range(p.layers):
        for r in range(p.back_part):
            rows = None
            for m in range(p.groups):
                at, source = divmod(
                    layer * p.own_cells + m * p.back_part + r, p.part_rows
                )[::-1]
                shift = (m - source) * p.width % LANES
                moved = pltpu.roll(rest[at], shift, 1) if shift else rest[at]
                rows = moved if rows is None else jnp.where(group == m, moved, rows)
            send(layer, p.back_tail + r, rows)


def mix_kernel(p, in_ref, weights_ref, *refs):
    out_refs, (x_ref, all_ref) = refs[: p.layers], refs[p.layers :]
    tiles = p.tiles
    in_ref = in_ref.reshape(tiles * p.layers * p.back_rows, LANES)
    shape = (tiles, LANES)
    pitch = p.layers * p.back_rows
    group = lane_group(shape, p.width)
    part = lax.broadcasted_iota(jnp.int32, shape, 0) % p.groups
    places = [(group == g) & (part == g) for g in range(p.groups)]

    def row(layer, at):
        return in_ref[pl.ds(layer * p.back_rows + at, tiles, stride=pitch), :]

    for r in range(p.back_part):
        turned = []
        for layer in range(p.layers):
            value = row(layer, p.back_tail + r)
            turned.append([value] + [pltpu.roll(value, s * p.width, 1) for s in range(1, p.groups)])
        for m in range(p.groups):
            own = m * p.back_part + r
            for layer in range(p.layers):
                base = layer * p.levels
                for f in range(p.full):
                    x_ref[own, pl.ds(base + f, tiles, stride=p.full), :] = row(
                        layer, f * p.own_cells + own
                    )
                tail = jnp.zeros(shape, jnp.float32)
                for g in range(p.groups):
                    tail = jnp.where(places[g], turned[layer][(g - m) % p.groups], tail)
                reach = 1
                while reach < p.groups:
                    tail = tail + pltpu.roll(tail, tiles - reach, 0)
                    reach *= 2
                for h in range(p.spare):
                    at = base + p.full * tiles + h
                    x_ref[own, at : at + 1, :] = tail[h * p.groups : h * p.groups + 1]
    for own in range(p.own_cells):
        x = x_ref[own]
        weights = weights_ref[own]
        scale = 0.4 / jnp.sum(weights, axis=-1, keepdims=True)
        x_high = x.astype(jnp.bfloat16)
        x_low = (x - x_high.astype(jnp.float32)).astype(jnp.bfloat16)
        w_high = weights.astype(jnp.bfloat16)
        w_low = (weights - w_high.astype(jnp.float32)).astype(jnp.bfloat16)
        dot = functools.partial(jnp.dot, preferred_element_type=jnp.float32)
        both = dot(w_high, jnp.concatenate([x_high, x_low], axis=1))
        total = both[:, :LANES] + (both[:, LANES:] + dot(w_low, x_high))
        all_ref[pl.ds(own, p.all_levels, stride=p.own_cells), :] = 0.6 * x + scale * total
    me = lax.axis_index("lev")
    size = p.levels * p.own_cells
    for s in range(p.layers):
        layer = lax.rem(me + s, p.layers)
        out_refs[s][...] = all_ref[pl.ds(pl.multiple_of(layer * size, SUBLANES), size), :]


def place_kernel(p, shifts, *refs):
    in_refs, out_ref, sems = refs[: len(shifts)], refs[-2], refs[-1]
    me = lax.axis_index("lev")
    tall = p.own_cells // p.side
    copies = []
    for n, s in enumerate(shifts):
        layer = lax.rem(me - s + p.layers, p.layers)
        piece = in_refs[n].reshape(p.levels, tall, p.side, LANES)
        for r in range(tall):
            copies.append(
                pltpu.make_async_copy(
                    piece.at[:, r], out_ref.at[layer * tall + r], sems.at[len(copies)]
                )
            )
            copies[-1].start()
    for copy in copies:
        copy.wait()


def in_vmem(count):
    return [pl.BlockSpec(memory_space=pltpu.VMEM)] * count


def params():
    return pltpu.CompilerParams(vmem_limit_bytes=VMEM_LIMIT)


def by_levels(p, tracers, courant_first, courant_second, weights, frame_flip):
    f32 = jnp.float32
    across = (p.side, p.levels, p.side, p.tracers)
    chips = p.tiles // 2
    blocks = (p.rows // p.side, p.side, LANES)
    *own, other = pl.pallas_call(
        functools.partial(pack_kernel, p),
        out_shape=[jax.ShapeDtypeStruct(blocks, f32)] * chips
        + [jax.ShapeDtypeStruct((chips,) + blocks, f32)],
        in_specs=[pl.BlockSpec(memory_space=pltpu.HBM)] * 4,
        out_specs=in_vmem(chips + 1),
        scratch_shapes=[
            pltpu.VMEM((p.side, p.spare, p.side, LANES), f32),
            pltpu.VMEM((2, p.side, p.side, p.levels), f32),
            pltpu.VMEM((1, 2), jnp.int32),
            pltpu.VMEM((LANES, LANES), f32),
            pltpu.VMEM((p.tiles, p.part_rows // p.side + 1, p.side, LANES), f32),
            pltpu.SemaphoreType.DMA((4 + p.tiles,)),
        ],
        compiler_params=params(),
        name="pack",
    )(
        *(
            pltpu.with_memory_space_constraint(value, pltpu.HBM)
            for value in (
                tracers[0].transpose(0, 2, 1, 3),
                courant_first[0],
                courant_second[0],
                frame_flip,
            )
        )
    )
    got = swapped(other, "tile", 1)
    pieces = [None] * p.tiles
    for s in range(chips - 1, -1, -1):
        for e, block in ((0, own[s]), (1, got[s])):
            block = block.reshape(p.rows, LANES)
            pieces[2 * s + e] = swapped(block, "tile", 2 * s) if s else block
    moved = pl.pallas_call(
        functools.partial(advect_kernel, p, tile_stride(p.tiles)),
        out_shape=jax.ShapeDtypeStruct(
            (p.tiles * p.layers, p.back_rows // FEW, FEW, LANES), f32
        ),
        in_specs=in_vmem(len(pieces)),
        out_specs=pl.BlockSpec(memory_space=pltpu.VMEM),
        scratch_shapes=[
            pltpu.VMEM((p.tiles * p.rows, LANES), f32),
            pltpu.VMEM((p.full * p.cells + p.part_rows, p.tiles, LANES), f32),
        ]
        + [pltpu.VMEM((2 * (p.full * p.cells + p.part_rows), p.tiles, LANES), f32)] * 3,
        compiler_params=params(),
        name="advect",
    )(*pieces)
    columns = lax.all_to_all(
        moved,
        ("tile", "lev"),
        split_axis=0,
        concat_axis=0,
        tiled=True,
    )
    size = p.levels * p.own_cells
    mixed = pl.pallas_call(
        functools.partial(mix_kernel, p),
        out_shape=[jax.ShapeDtypeStruct((size, LANES), f32)] * p.layers,
        in_specs=in_vmem(2),
        out_specs=in_vmem(p.layers),
        scratch_shapes=[
            pltpu.VMEM((p.own_cells, p.all_levels, LANES), f32),
            pltpu.VMEM((p.all_levels * p.own_cells, LANES), f32),
        ],
        compiler_params=params(),
        name="mix",
    )(
        columns,
        weights.reshape(p.own_cells, p.all_levels, p.all_levels),
    )
    pieces = [mixed[0]] + [passed_along(mixed[s], "lev", s) for s in range(1, p.layers)]
    order = sorted(range(p.layers), key=lambda s: -min(s, p.layers - s) if s else -p.layers)
    placed = None
    for shifts in (order[:2], order[2:]):
        before = [] if placed is None else [placed]
        placed = pl.pallas_call(
            functools.partial(place_kernel, p, shifts),
            out_shape=jax.ShapeDtypeStruct(across, f32),
            in_specs=in_vmem(len(shifts))
            + [pl.BlockSpec(memory_space=pltpu.HBM)] * len(before),
            out_specs=pl.BlockSpec(memory_space=pltpu.HBM),
            scratch_shapes=[
                pltpu.SemaphoreType.DMA((len(shifts) * p.own_cells // p.side,))
            ],
            input_output_aliases={len(shifts): 0} if before else {},
            compiler_params=params(),
            name="place",
        )(*(pieces[s] for s in shifts), *before)
    return placed.transpose(0, 2, 1, 3)[None]


def on_device(tracers, courant_first, courant_second, weights, frame_flip):
    plan = Plan(
        tracers.shape[1],
        tracers.shape[3],
        tracers.shape[4],
        lax.axis_size("tile"),
        lax.axis_size("lev"),
    )
    if tracers.shape[1] == tracers.shape[2] and tracers.shape[0] == 1 and plan.fits:
        return by_levels(plan, tracers, courant_first, courant_second, weights, frame_flip)
    return by_halos(tracers, courant_first, courant_second, weights, frame_flip)


def solution(mesh):
    in_specs = (
        P("tile", None, None, "lev", None),
        P("tile", None, None, "lev"),
        P("tile", None, None, "lev"),
        P("tile", "lev", None, None, None),
        P("tile", None),
    )
    out_specs = P("tile", None, None, "lev", None)
    return jax.shard_map(
        on_device, mesh=mesh, in_specs=in_specs, out_specs=out_specs, check_vma=False
    )
```

```python
import functools

import jax
import jax.numpy as jnp
from jax import lax
from jax.experimental import pallas as pl
from jax.experimental.pallas import tpu as pltpu
from jax.sharding import PartitionSpec as P

SUBSTEPS = 3
SUBLANES = 8
LANES = 128
FEW = 4
VMEM_LIMIT = 40 * 1024 * 1024


def passed_along(value, axis, steps):
    count = lax.axis_size(axis)
    pairs = [(source, (source + steps) % count) for source in range(count)]
    return lax.ppermute(value, axis, pairs)


def ppm_update(extended, courant, along):
    length = extended.shape[along] - 6

    def window(values, offset, amount):
        return lax.slice_in_dim(values, offset, offset + amount, axis=along)

    interfaces = (
        7.0 * (window(extended, 1, length + 3) + window(extended, 2, length + 3))
        - (window(extended, 0, length + 3) + window(extended, 3, length + 3))
    ) / 12.0
    low_edge = window(interfaces, 0, length + 2)
    high_edge = window(interfaces, 1, length + 2)
    centre = window(extended, 2, length + 2)
    gradient = high_edge - low_edge
    curvature = 6.0 * centre - 3.0 * (low_edge + high_edge)
    upward = courant * (
        window(high_edge, 0, length + 1)
        - 0.5
        * courant
        * (
            window(gradient, 0, length + 1)
            - (1.0 - courant * (2.0 / 3.0)) * window(curvature, 0, length + 1)
        )
    )
    downward = courant * (
        window(low_edge, 1, length + 1)
        - 0.5
        * courant
        * (
            window(gradient, 1, length + 1)
            + (1.0 + courant * (2.0 / 3.0)) * window(curvature, 1, length + 1)
        )
    )
    fluxes = jnp.where(courant >= 0.0, upward, downward)
    return window(centre, 1, length) - (window(fluxes, 1, length) - window(fluxes, 0, length))


def to_frame(blocks, flip_flags):
    first_flag = (flip_flags[:, 0] == 1)[:, None, None, None, None]
    second_flag = (flip_flags[:, 1] == 1)[:, None, None, None, None]
    turned = jnp.where(first_flag, blocks[:, ::-1], blocks)
    return jnp.where(second_flag, turned[:, :, ::-1], turned)


def mixing_matrix(weights):
    totals = jnp.sum(weights, axis=-1, keepdims=True)
    identity = jnp.eye(weights.shape[-1], dtype=jnp.float32)
    return 0.6 * identity + 0.4 * (weights / totals)


def swapped(value, axis, mask):
    pairs = [(source, source ^ mask) for source in range(lax.axis_size(axis))]
    return lax.ppermute(value, axis, pairs)


def tile_stride(tiles):
    return max(2, tiles // 8)


def by_halos(tracers, courant_first, courant_second, weights, frame_flip):
    stride = tile_stride(lax.axis_size("tile"))
    extent = tracers.shape[1]
    fields = to_frame(tracers, frame_flip)
    first_faces = courant_first[..., None]
    second_faces = courant_second[..., None]
    for substep in range(SUBSTEPS):
        for along, faces, steps in ((1, first_faces, stride), (2, second_faces, 1)):
            size = fields.shape[along]
            high_cells = lax.slice_in_dim(fields, size - 3, size, axis=along)
            low_cells = lax.slice_in_dim(fields, 0, 3, axis=along)
            high_face = lax.slice_in_dim(faces, size - 1, size, axis=along)
            from_low, low_face = passed_along((high_cells, high_face), "tile", steps)
            from_high = passed_along(low_cells, "tile", -steps)
            fields = ppm_update(
                jnp.concatenate([from_low, fields, from_high], axis=along),
                jnp.concatenate([low_face, faces], axis=along),
                along,
            )
    advected = to_frame(fields, frame_flip)
    mixing = mixing_matrix(weights)
    columns = lax.all_to_all(advected, "lev", split_axis=1, concat_axis=3, tiled=True)
    mixed = jnp.einsum("txykl,txylq->txykq", mixing, columns, precision=lax.Precision.HIGHEST)
    return lax.all_to_all(mixed, "lev", split_axis=3, concat_axis=1, tiled=True)


class Plan:
    def __init__(self, side, levels, tracers, tiles, layers):
        self.side, self.levels, self.tracers = side, levels, tracers
        self.tiles, self.layers = tiles, layers
        self.cells = side * side
        self.full = levels // tiles
        self.spare = levels - self.full * tiles
        self.fits = (
            tiles == SUBLANES
            and tracers == LANES
            and self.cells * 2 == LANES
            and side % layers == 0
            and self.spare > 0
            and self.full > 0
            and tiles % self.spare == 0
        )
        if not self.fits:
            return
        self.groups = tiles // self.spare
        self.width = tracers // self.groups
        self.part_rows = self.cells // self.groups
        self.kinds = self.full + 1
        self.tail_at = self.full * self.cells
        self.courant_at = self.tail_at + self.part_rows
        self.flip_at = self.courant_at + self.kinds
        self.rows = -(-(self.flip_at + 1) // SUBLANES) * SUBLANES
        self.own_cells = self.cells // layers
        self.back_tail = self.full * self.own_cells
        self.back_part = self.own_cells // self.groups
        self.back_rows = self.back_tail + self.back_part
        self.all_levels = levels * layers
        self.fits = (
            self.cells % self.groups == 0
            and self.own_cells % self.groups == 0
            and self.part_rows % (2 * side) == 0
            and self.side == SUBLANES
            and self.own_cells % side == 0
            and self.kinds < SUBLANES
            and self.back_rows % FEW == 0
        )


def lane_group(shape, width):
    return lax.broadcasted_iota(jnp.int32, shape, 1) // width


def pack_kernel(p, x_ref, first_ref, second_ref, flip_ref, *refs):
    chips = p.tiles // 2
    own_refs, other_ref = refs[:chips], refs[chips]
    spare_ref, courant_ref, flags_ref, faces_ref, rest_ref, sems = refs[chips + 1 :]
    me = lax.axis_index("tile")
    slots = []
    for s in range(chips):
        slots.append((lax.bitwise_xor(me, 2 * s), own_refs[s]))
        slots.append((lax.bitwise_xor(me, 2 * s + 1), other_ref.at[s]))
    copies = []

    def fetch(source, target):
        copy = pltpu.make_async_copy(source, target, sems.at[len(copies)])
        copy.start()
        copies.append(copy)

    for source, target in ((first_ref, courant_ref.at[0]), (second_ref, courant_ref.at[1])):
        fetch(source, target)
    fetch(flip_ref, flags_ref)
    fetch(x_ref.at[:, pl.ds(p.full * p.tiles, p.spare)], spare_ref)
    small = 3
    for d, slot in slots:
        fetch(
            x_ref.at[:, pl.ds(p.full * d, p.full)],
            slot.at[pl.ds(0, p.full * p.side)].reshape(p.side, p.full, p.side, LANES),
        )
    filler = jnp.zeros((p.side, LANES), jnp.float32)
    group = lane_group((p.side, LANES), p.width)
    copies[small].wait()
    tall = p.part_rows // p.side
    for h in range(p.spare):
        for g in range(p.groups):
            for r in range(tall):
                rows = None
                for m in range(p.groups):
                    part = spare_ref[m * tall + r, h]
                    shift = (m - g) * p.width % LANES
                    moved = pltpu.roll(part, shift, 1) if shift else part
                    rows = moved if rows is None else jnp.where(group == m, moved, rows)
                rest_ref[h * p.groups + g, r] = rows
    for copy in copies[:small]:
        copy.wait()
    for way in range(2):
        for i in range(p.side):
            at = way * p.cells + i * p.side
            faces_ref[at : at + p.side, :] = filler
            faces_ref[at : at + p.side, : p.levels] = courant_ref[way, i]
    faces = faces_ref[...].T
    lane = lax.broadcasted_iota(jnp.int32, (1, LANES), 1)
    flags = flags_ref[...].astype(jnp.float32)
    flips = jnp.where(
        lane < p.cells,
        jnp.broadcast_to(flags[:, 0:1], (1, LANES)),
        jnp.broadcast_to(flags[:, 1:2], (1, LANES)),
    )
    for d in range(p.tiles):
        level = p.full * d
        rest = p.full * p.tiles + d // p.groups
        rest_ref[d, tall] = filler
        rest_ref[d, tall, : p.full, :] = faces[level : level + p.full]
        rest_ref[d, tall, p.full : p.kinds, :] = faces[rest : rest + 1]
        rest_ref[d, tall, p.kinds : p.kinds + 1, :] = flips
    for d, slot in slots:
        for r in range(tall + 1):
            slot[p.full * p.side + r] = rest_ref[d, r]
    for copy in copies[small + 1 :]:
        copy.wait()


def advect_kernel(p, stride, *refs):
    tiles, side, cells = p.tiles, p.side, p.cells
    shape = (tiles, LANES)
    parts = refs[: -6]
    out_ref, in_ref, q_ref, near_ref, far_ref, mid_ref = refs[-6:]
    out_ref = out_ref.reshape(tiles * p.layers * p.back_rows, LANES)
    me = lax.axis_index("tile")
    each = tiles // len(parts)
    for s, part in enumerate(parts):
        for e in range(each):
            tile = lax.bitwise_xor(me, s * each + e)
            in_ref[pl.ds(pl.multiple_of(tile * p.rows, SUBLANES), p.rows), :] = part[
                e * p.rows : (e + 1) * p.rows, :
            ]

    def row(at):
        return in_ref[pl.ds(at, tiles, stride=p.rows), :]

    flips = row(p.flip_at)
    first_flip = jnp.broadcast_to(flips[:, 0:1], shape) > 0.5
    second_flip = jnp.broadcast_to(flips[:, cells : cells + 1], shape) > 0.5
    group = lane_group(shape, p.width)
    tall = p.part_rows // side

    def reversed_groups(value):
        turned = {}
        result = None
        for g in range(p.groups):
            by = (2 * g + 1) % p.groups
            if by not in turned:
                turned[by] = pltpu.roll(value, by * p.width, 1) if by else value
            result = turned[by] if result is None else jnp.where(group == g, turned[by], result)
        return result

    def mirrored(get, height, back):
        for i in range(height // 2):
            for j in range(side // 2):
                i2, j2 = height - 1 - i, side - 1 - j
                ll, hl, lh, hh = get(i, j), get(i2, j), get(i, j2), get(i2, j2)
                a, b = jnp.where(first_flip, back(hl), ll), jnp.where(first_flip, back(ll), hl)
                c, d = jnp.where(first_flip, back(hh), lh), jnp.where(first_flip, back(lh), hh)
                yield i * side + j, jnp.where(second_flip, c, a)
                yield i2 * side + j, jnp.where(second_flip, d, b)
                yield i * side + j2, jnp.where(second_flip, a, c)
                yield i2 * side + j2, jnp.where(second_flip, b, d)

    def plain(value):
        return value

    def set_faces(at, c):
        e = jnp.abs(c)
        u = 1.0 - e
        cu = c * u
        near_ref[at] = (cu * u) * (1.0 / 12.0)
        far_ref[at] = (cu * e) * (-1.0 / 12.0)
        mid_ref[at] = (c * e) * (3.0 - 2.0 * e)

    tail = p.full * cells
    tail_faces = p.full * 2 * cells
    for kind in range(p.full):
        for cell, value in mirrored(
            lambda i, j: row((i * p.full + kind) * side + j), side, plain
        ):
            q_ref[kind * cells + cell] = value
        courant = row(p.courant_at + kind)
        for at in range(2 * cells):
            set_faces(kind * 2 * cells + at, jnp.broadcast_to(courant[:, at : at + 1], shape))
    for cell, value in mirrored(
        lambda i, j: row(p.tail_at + i * side + j), tall, reversed_groups
    ):
        q_ref[tail + cell] = value
    courant = row(p.courant_at + p.full)
    for way in range(2):
        for r in range(p.part_rows):
            at = group * p.part_rows + (way * cells + r)
            c = jnp.take_along_axis(courant, at, axis=1)
            set_faces(tail_faces + way * p.part_rows + r, c)

    def sweep(at, faces_at, step, length, up, down):
        cell = [at + step * i for i in range(length)]
        face = [faces_at + step * i for i in range(length)]
        q = [q_ref[cell[i]] for i in range(length)]
        ext = [up(q[length - 1])] + q + [down(q[0]), down(q[1])]
        edge = [
            7.0 * (ext[i + 1] + ext[i + 2]) - (ext[i] + ext[i + 3]) for i in range(length)
        ]
        edges = [up(edge[length - 1])] + edge + [down(edge[0])]
        flux = []
        for i in range(length):
            near = near_ref[face[i]]
            upwind = near >= 0.0
            far = jnp.where(upwind, edges[i], edges[i + 2])
            mid = jnp.where(upwind, ext[i + 1], ext[i + 2])
            flux.append(near * edge[i] + far_ref[face[i]] * far + mid_ref[face[i]] * mid)
        fluxes = [up(flux[length - 1])] + flux
        for i in range(length):
            q_ref[cell[i]] = q[i] - (fluxes[i + 1] - fluxes[i])

    def low_tile(shift):
        return lambda v: pltpu.roll(v, shift, 0)

    def high_tile(shift):
        return lambda v: pltpu.roll(v, tiles - shift, 0)

    def low_group(v):
        moved = pltpu.roll(v, p.width, 1)
        return jnp.where(group == 0, low_tile(stride)(moved), moved)

    def high_group(v):
        moved = pltpu.roll(v, LANES - p.width, 1)
        return jnp.where(group == p.groups - 1, high_tile(stride)(moved), moved)

    def step(count, carry):
        for j in range(side):
            for kind in range(p.full):
                at, faces_at = kind * cells + j, kind * 2 * cells + j
                sweep(at, faces_at, side, side, low_tile(stride), high_tile(stride))
            sweep(tail + j, tail_faces + j, side, tall, low_group, high_group)
        for i in range(side):
            for kind in range(p.full):
                at, faces_at = kind * cells + i * side, (kind * 2 + 1) * cells + i * side
                sweep(at, faces_at, 1, side, low_tile(1), high_tile(1))
            if i < tall:
                at, faces_at = tail + i * side, tail_faces + p.part_rows + i * side
                sweep(at, faces_at, 1, side, low_tile(1), high_tile(1))
        return carry

    lax.fori_loop(0, SUBSTEPS, step, 0)

    pitch = p.layers * p.back_rows

    def send(layer, at, value):
        out_ref[pl.ds(layer * p.back_rows + at, tiles, stride=pitch), :] = value

    for kind in range(p.full):
        for cell, value in mirrored(
            lambda i, j: q_ref[kind * cells + i * side + j], side, plain
        ):
            layer, own = divmod(cell, p.own_cells)
            send(layer, kind * p.own_cells + own, value)
    rest = dict(mirrored(lambda i, j: q_ref[tail + i * side + j], tall, reversed_groups))
    for layer in range(p.layers):
        for r in range(p.back_part):
            rows = None
            for m in range(p.groups):
                at, source = divmod(
                    layer * p.own_cells + m * p.back_part + r, p.part_rows
                )[::-1]
                shift = (m - source) * p.width % LANES
                moved = pltpu.roll(rest[at], shift, 1) if shift else rest[at]
                rows = moved if rows is None else jnp.where(group == m, moved, rows)
            send(layer, p.back_tail + r, rows)


def mix_kernel(p, in_ref, weights_ref, *refs):
    out_refs, (x_ref, all_ref) = refs[: p.layers], refs[p.layers :]
    tiles = p.tiles
    in_ref = in_ref.reshape(tiles * p.layers * p.back_rows, LANES)
    shape = (tiles, LANES)
    pitch = p.layers * p.back_rows
    group = lane_group(shape, p.width)
    part = lax.broadcasted_iota(jnp.int32, shape, 0) % p.groups
    places = [(group == g) & (part == g) for g in range(p.groups)]

    def row(layer, at):
        return in_ref[pl.ds(layer * p.back_rows + at, tiles, stride=pitch), :]

    for r in range(p.back_part):
        turned = []
        for layer in range(p.layers):
            value = row(layer, p.back_tail + r)
            turned.append([value] + [pltpu.roll(value, s * p.width, 1) for s in range(1, p.groups)])
        for m in range(p.groups):
            own = m * p.back_part + r
            for layer in range(p.layers):
                base = layer * p.levels
                for f in range(p.full):
                    x_ref[own, pl.ds(base + f, tiles, stride=p.full), :] = row(
                        layer, f * p.own_cells + own
                    )
                tail = jnp.zeros(shape, jnp.float32)
                for g in range(p.groups):
                    tail = jnp.where(places[g], turned[layer][(g - m) % p.groups], tail)
                reach = 1
                while reach < p.groups:
                    tail = tail + pltpu.roll(tail, tiles - reach, 0)
                    reach *= 2
                for h in range(p.spare):
                    at = base + p.full * tiles + h
                    x_ref[own, at : at + 1, :] = tail[h * p.groups : h * p.groups + 1]
    for own in range(p.own_cells):
        x = x_ref[own]
        weights = weights_ref[own]
        scale = 0.4 / jnp.sum(weights, axis=-1, keepdims=True)
        x_high = x.astype(jnp.bfloat16)
        x_low = (x - x_high.astype(jnp.float32)).astype(jnp.bfloat16)
        w_high = weights.astype(jnp.bfloat16)
        w_low = (weights - w_high.astype(jnp.float32)).astype(jnp.bfloat16)
        dot = functools.partial(jnp.dot, preferred_element_type=jnp.float32)
        both = dot(w_high, jnp.concatenate([x_high, x_low], axis=1))
        total = both[:, :LANES] + (both[:, LANES:] + dot(w_low, x_high))
        all_ref[pl.ds(own, p.all_levels, stride=p.own_cells), :] = 0.6 * x + scale * total
    me = lax.axis_index("lev")
    size = p.levels * p.own_cells
    for s in range(p.layers):
        layer = lax.rem(me + s, p.layers)
        out_refs[s][...] = all_ref[pl.ds(pl.multiple_of(layer * size, SUBLANES), size), :]


def place_kernel(p, shifts, *refs):
    in_refs, out_ref, sems = refs[: len(shifts)], refs[-2], refs[-1]
    me = lax.axis_index("lev")
    tall = p.own_cells // p.side
    copies = []
    for n, s in enumerate(shifts):
        layer = lax.rem(me - s + p.layers, p.layers)
        piece = in_refs[n].reshape(p.levels, tall, p.side, LANES)
        for r in range(tall):
            copies.append(
                pltpu.make_async_copy(
                    piece.at[:, r], out_ref.at[layer * tall + r], sems.at[len(copies)]
                )
            )
            copies[-1].start()
    for copy in copies:
        copy.wait()


def in_vmem(count):
    return [pl.BlockSpec(memory_space=pltpu.VMEM)] * count


def params():
    return pltpu.CompilerParams(vmem_limit_bytes=VMEM_LIMIT)


def by_levels(p, tracers, courant_first, courant_second, weights, frame_flip):
    f32 = jnp.float32
    across = (p.side, p.levels, p.side, p.tracers)
    chips = p.tiles // 2
    blocks = (p.rows // p.side, p.side, LANES)
    *own, other = pl.pallas_call(
        functools.partial(pack_kernel, p),
        out_shape=[jax.ShapeDtypeStruct(blocks, f32)] * chips
        + [jax.ShapeDtypeStruct((chips,) + blocks, f32)],
        in_specs=[pl.BlockSpec(memory_space=pltpu.HBM)] * 4,
        out_specs=in_vmem(chips + 1),
        scratch_shapes=[
            pltpu.VMEM((p.side, p.spare, p.side, LANES), f32),
            pltpu.VMEM((2, p.side, p.side, p.levels), f32),
            pltpu.VMEM((1, 2), jnp.int32),
            pltpu.VMEM((LANES, LANES), f32),
            pltpu.VMEM((p.tiles, p.part_rows // p.side + 1, p.side, LANES), f32),
            pltpu.SemaphoreType.DMA((4 + p.tiles,)),
        ],
        compiler_params=params(),
        name="pack",
    )(
        *(
            pltpu.with_memory_space_constraint(value, pltpu.HBM)
            for value in (
                tracers[0].transpose(0, 2, 1, 3),
                courant_first[0],
                courant_second[0],
                frame_flip,
            )
        )
    )
    got = swapped(other, "tile", 1)
    pieces = [None] * p.tiles
    for s in range(chips - 1, -1, -1):
        for e, block in ((0, own[s]), (1, got[s])):
            block = block.reshape(p.rows, LANES)
            pieces[2 * s + e] = swapped(block, "tile", 2 * s) if s else block
    moved = pl.pallas_call(
        functools.partial(advect_kernel, p, tile_stride(p.tiles)),
        out_shape=jax.ShapeDtypeStruct(
            (p.tiles * p.layers, p.back_rows // FEW, FEW, LANES), f32
        ),
        in_specs=in_vmem(len(pieces)),
        out_specs=pl.BlockSpec(memory_space=pltpu.VMEM),
        scratch_shapes=[
            pltpu.VMEM((p.tiles * p.rows, LANES), f32),
            pltpu.VMEM((p.full * p.cells + p.part_rows, p.tiles, LANES), f32),
        ]
        + [pltpu.VMEM((2 * (p.full * p.cells + p.part_rows), p.tiles, LANES), f32)] * 3,
        compiler_params=params(),
        name="advect",
    )(*pieces)
    columns = lax.all_to_all(
        moved,
        ("tile", "lev"),
        split_axis=0,
        concat_axis=0,
        tiled=True,
    )
    size = p.levels * p.own_cells
    mixed = pl.pallas_call(
        functools.partial(mix_kernel, p),
        out_shape=[jax.ShapeDtypeStruct((size, LANES), f32)] * p.layers,
        in_specs=in_vmem(2),
        out_specs=in_vmem(p.layers),
        scratch_shapes=[
            pltpu.VMEM((p.own_cells, p.all_levels, LANES), f32),
            pltpu.VMEM((p.all_levels * p.own_cells, LANES), f32),
        ],
        compiler_params=params(),
        name="mix",
    )(
        columns,
        weights.reshape(p.own_cells, p.all_levels, p.all_levels),
    )
    pieces = [mixed[0]] + [passed_along(mixed[s], "lev", s) for s in range(1, p.layers)]
    order = sorted(range(p.layers), key=lambda s: -min(s, p.layers - s) if s else -p.layers)
    placed = None
    for shifts in (order[:2], order[2:]):
        before = [] if placed is None else [placed]
        placed = pl.pallas_call(
            functools.partial(place_kernel, p, shifts),
            out_shape=jax.ShapeDtypeStruct(across, f32),
            in_specs=in_vmem(len(shifts))
            + [pl.BlockSpec(memory_space=pltpu.HBM)] * len(before),
            out_specs=pl.BlockSpec(memory_space=pltpu.HBM),
            scratch_shapes=[
                pltpu.SemaphoreType.DMA((len(shifts) * p.own_cells // p.side,))
            ],
            input_output_aliases={len(shifts): 0} if before else {},
            compiler_params=params(),
            name="place",
        )(*(pieces[s] for s in shifts), *before)
    return placed.transpose(0, 2, 1, 3)[None]


def on_device(tracers, courant_first, courant_second, weights, frame_flip):
    plan = Plan(
        tracers.shape[1],
        tracers.shape[3],
        tracers.shape[4],
        lax.axis_size("tile"),
        lax.axis_size("lev"),
    )
    if tracers.shape[1] == tracers.shape[2] and tracers.shape[0] == 1 and plan.fits:
        return by_levels(plan, tracers, courant_first, courant_second, weights, frame_flip)
    return by_halos(tracers, courant_first, courant_second, weights, frame_flip)


def solution(mesh):
    in_specs = (
        P("tile", None, None, "lev", None),
        P("tile", None, None, "lev"),
        P("tile", None, None, "lev"),
        P("tile", "lev", None, None, None),
        P("tile", None),
    )
    out_specs = P("tile", None, None, "lev", None)
    return jax.shard_map(
        on_device, mesh=mesh, in_specs=in_specs, out_specs=out_specs, check_vma=False
    )
```

```python
import functools

import jax
import jax.numpy as jnp
from jax import lax
from jax.experimental import pallas as pl
from jax.experimental.pallas import tpu as pltpu
from jax.sharding import PartitionSpec as P

SUBSTEPS = 3
SUBLANES = 8
LANES = 128
FEW = 4
VMEM_LIMIT = 40 * 1024 * 1024


def passed_along(value, axis, steps):
    count = lax.axis_size(axis)
    pairs = [(source, (source + steps) % count) for source in range(count)]
    return lax.ppermute(value, axis, pairs)


def ppm_update(extended, courant, along):
    length = extended.shape[along] - 6

    def window(values, offset, amount):
        return lax.slice_in_dim(values, offset, offset + amount, axis=along)

    interfaces = (
        7.0 * (window(extended, 1, length + 3) + window(extended, 2, length + 3))
        - (window(extended, 0, length + 3) + window(extended, 3, length + 3))
    ) / 12.0
    low_edge = window(interfaces, 0, length + 2)
    high_edge = window(interfaces, 1, length + 2)
    centre = window(extended, 2, length + 2)
    gradient = high_edge - low_edge
    curvature = 6.0 * centre - 3.0 * (low_edge + high_edge)
    upward = courant * (
        window(high_edge, 0, length + 1)
        - 0.5
        * courant
        * (
            window(gradient, 0, length + 1)
            - (1.0 - courant * (2.0 / 3.0)) * window(curvature, 0, length + 1)
        )
    )
    downward = courant * (
        window(low_edge, 1, length + 1)
        - 0.5
        * courant
        * (
            window(gradient, 1, length + 1)
            + (1.0 + courant * (2.0 / 3.0)) * window(curvature, 1, length + 1)
        )
    )
    fluxes = jnp.where(courant >= 0.0, upward, downward)
    return window(centre, 1, length) - (window(fluxes, 1, length) - window(fluxes, 0, length))


def to_frame(blocks, flip_flags):
    first_flag = (flip_flags[:, 0] == 1)[:, None, None, None, None]
    second_flag = (flip_flags[:, 1] == 1)[:, None, None, None, None]
    turned = jnp.where(first_flag, blocks[:, ::-1], blocks)
    return jnp.where(second_flag, turned[:, :, ::-1], turned)


def mixing_matrix(weights):
    totals = jnp.sum(weights, axis=-1, keepdims=True)
    identity = jnp.eye(weights.shape[-1], dtype=jnp.float32)
    return 0.6 * identity + 0.4 * (weights / totals)


def swapped(value, axis, mask):
    pairs = [(source, source ^ mask) for source in range(lax.axis_size(axis))]
    return lax.ppermute(value, axis, pairs)


def tile_stride(tiles):
    return max(2, tiles // 8)


def by_halos(tracers, courant_first, courant_second, weights, frame_flip):
    stride = tile_stride(lax.axis_size("tile"))
    extent = tracers.shape[1]
    fields = to_frame(tracers, frame_flip)
    first_faces = courant_first[..., None]
    second_faces = courant_second[..., None]
    for substep in range(SUBSTEPS):
        for along, faces, steps in ((1, first_faces, stride), (2, second_faces, 1)):
            size = fields.shape[along]
            high_cells = lax.slice_in_dim(fields, size - 3, size, axis=along)
            low_cells = lax.slice_in_dim(fields, 0, 3, axis=along)
            high_face = lax.slice_in_dim(faces, size - 1, size, axis=along)
            from_low, low_face = passed_along((high_cells, high_face), "tile", steps)
            from_high = passed_along(low_cells, "tile", -steps)
            fields = ppm_update(
                jnp.concatenate([from_low, fields, from_high], axis=along),
                jnp.concatenate([low_face, faces], axis=along),
                along,
            )
    advected = to_frame(fields, frame_flip)
    mixing = mixing_matrix(weights)
    columns = lax.all_to_all(advected, "lev", split_axis=1, concat_axis=3, tiled=True)
    mixed = jnp.einsum("txykl,txylq->txykq", mixing, columns, precision=lax.Precision.HIGHEST)
    return lax.all_to_all(mixed, "lev", split_axis=3, concat_axis=1, tiled=True)


class Plan:
    def __init__(self, side, levels, tracers, tiles, layers):
        self.side, self.levels, self.tracers = side, levels, tracers
        self.tiles, self.layers = tiles, layers
        self.cells = side * side
        self.full = levels // tiles
        self.spare = levels - self.full * tiles
        self.fits = (
            tiles == SUBLANES
            and tracers == LANES
            and self.cells * 2 == LANES
            and side % layers == 0
            and self.spare > 0
            and self.full > 0
            and tiles % self.spare == 0
        )
        if not self.fits:
            return
        self.groups = tiles // self.spare
        self.width = tracers // self.groups
        self.part_rows = self.cells // self.groups
        self.kinds = self.full + 1
        self.tail_at = self.full * self.cells
        self.courant_at = self.tail_at + self.part_rows
        self.flip_at = self.courant_at + self.kinds
        self.rows = -(-(self.flip_at + 1) // SUBLANES) * SUBLANES
        self.own_cells = self.cells // layers
        self.back_tail = self.full * self.own_cells
        self.back_part = self.own_cells // self.groups
        self.back_rows = self.back_tail + self.back_part
        self.all_levels = levels * layers
        self.fits = (
            self.cells % self.groups == 0
            and self.own_cells % self.groups == 0
            and self.part_rows % (2 * side) == 0
            and self.side == SUBLANES
            and self.own_cells % side == 0
            and self.kinds < SUBLANES
            and self.back_rows % FEW == 0
        )


def lane_group(shape, width):
    return lax.broadcasted_iota(jnp.int32, shape, 1) // width


def pack_kernel(p, x_ref, first_ref, second_ref, flip_ref, *refs):
    chips = p.tiles // 2
    own_refs, other_ref = refs[:chips], refs[chips]
    spare_ref, courant_ref, flags_ref, faces_ref, rest_ref, sems = refs[chips + 1 :]
    me = lax.axis_index("tile")
    slots = []
    for s in range(chips):
        slots.append((lax.bitwise_xor(me, 2 * s), own_refs[s]))
        slots.append((lax.bitwise_xor(me, 2 * s + 1), other_ref.at[s]))
    copies = []

    def fetch(source, target):
        copy = pltpu.make_async_copy(source, target, sems.at[len(copies)])
        copy.start()
        copies.append(copy)

    for source, target in ((first_ref, courant_ref.at[0]), (second_ref, courant_ref.at[1])):
        fetch(source, target)
    fetch(flip_ref, flags_ref)
    fetch(x_ref.at[:, pl.ds(p.full * p.tiles, p.spare)], spare_ref)
    small = 3
    for d, slot in slots:
        fetch(
            x_ref.at[:, pl.ds(p.full * d, p.full)],
            slot.at[pl.ds(0, p.full * p.side)].reshape(p.side, p.full, p.side, LANES),
        )
    filler = jnp.zeros((p.side, LANES), jnp.float32)
    group = lane_group((p.side, LANES), p.width)
    copies[small].wait()
    tall = p.part_rows // p.side
    for h in range(p.spare):
        for g in range(p.groups):
            for r in range(tall):
                rows = None
                for m in range(p.groups):
                    part = spare_ref[m * tall + r, h]
                    shift = (m - g) * p.width % LANES
                    moved = pltpu.roll(part, shift, 1) if shift else part
                    rows = moved if rows is None else jnp.where(group == m, moved, rows)
                rest_ref[h * p.groups + g, r] = rows
    for copy in copies[:small]:
        copy.wait()
    for way in range(2):
        for i in range(p.side):
            at = way * p.cells + i * p.side
            faces_ref[at : at + p.side, :] = filler
            faces_ref[at : at + p.side, : p.levels] = courant_ref[way, i]
    faces = faces_ref[...].T
    lane = lax.broadcasted_iota(jnp.int32, (1, LANES), 1)
    flags = flags_ref[...].astype(jnp.float32)
    flips = jnp.where(
        lane < p.cells,
        jnp.broadcast_to(flags[:, 0:1], (1, LANES)),
        jnp.broadcast_to(flags[:, 1:2], (1, LANES)),
    )
    for d in range(p.tiles):
        level = p.full * d
        rest = p.full * p.tiles + d // p.groups
        rest_ref[d, tall] = filler
        rest_ref[d, tall, : p.full, :] = faces[level : level + p.full]
        rest_ref[d, tall, p.full : p.kinds, :] = faces[rest : rest + 1]
        rest_ref[d, tall, p.kinds : p.kinds + 1, :] = flips
    for d, slot in slots:
        for r in range(tall + 1):
            slot[p.full * p.side + r] = rest_ref[d, r]
    for copy in copies[small + 1 :]:
        copy.wait()


def advect_kernel(p, stride, *refs):
    tiles, side, cells = p.tiles, p.side, p.cells
    shape = (tiles, LANES)
    parts = refs[: -6]
    out_ref, in_ref, q_ref, near_ref, far_ref, mid_ref = refs[-6:]
    out_ref = out_ref.reshape(tiles * p.layers * p.back_rows, LANES)
    me = lax.axis_index("tile")
    each = tiles // len(parts)
    for s, part in enumerate(parts):
        for e in range(each):
            tile = lax.bitwise_xor(me, s * each + e)
            in_ref[pl.ds(pl.multiple_of(tile * p.rows, SUBLANES), p.rows), :] = part[
                e * p.rows : (e + 1) * p.rows, :
            ]

    def row(at):
        return in_ref[pl.ds(at, tiles, stride=p.rows), :]

    flips = row(p.flip_at)
    first_flip = jnp.broadcast_to(flips[:, 0:1], shape) > 0.5
    second_flip = jnp.broadcast_to(flips[:, cells : cells + 1], shape) > 0.5
    group = lane_group(shape, p.width)
    tall = p.part_rows // side

    def reversed_groups(value):
        turned = {}
        result = None
        for g in range(p.groups):
            by = (2 * g + 1) % p.groups
            if by not in turned:
                turned[by] = pltpu.roll(value, by * p.width, 1) if by else value
            result = turned[by] if result is None else jnp.where(group == g, turned[by], result)
        return result

    def mirrored(get, height, back):
        for i in range(height // 2):
            for j in range(side // 2):
                i2, j2 = height - 1 - i, side - 1 - j
                ll, hl, lh, hh = get(i, j), get(i2, j), get(i, j2), get(i2, j2)
                a, b = jnp.where(first_flip, back(hl), ll), jnp.where(first_flip, back(ll), hl)
                c, d = jnp.where(first_flip, back(hh), lh), jnp.where(first_flip, back(lh), hh)
                yield i * side + j, jnp.where(second_flip, c, a)
                yield i2 * side + j, jnp.where(second_flip, d, b)
                yield i * side + j2, jnp.where(second_flip, a, c)
                yield i2 * side + j2, jnp.where(second_flip, b, d)

    def plain(value):
        return value

    def set_faces(at, c):
        e = jnp.abs(c)
        u = 1.0 - e
        cu = c * u
        near_ref[at] = (cu * u) * (1.0 / 12.0)
        far_ref[at] = (cu * e) * (-1.0 / 12.0)
        mid_ref[at] = (c * e) * (3.0 - 2.0 * e)

    tail = p.full * cells
    tail_faces = p.full * 2 * cells
    for kind in range(p.full):
        for cell, value in mirrored(
            lambda i, j: row((i * p.full + kind) * side + j), side, plain
        ):
            q_ref[kind * cells + cell] = value
        courant = row(p.courant_at + kind)
        for at in range(2 * cells):
            set_faces(kind * 2 * cells + at, jnp.broadcast_to(courant[:, at : at + 1], shape))
    for cell, value in mirrored(
        lambda i, j: row(p.tail_at + i * side + j), tall, reversed_groups
    ):
        q_ref[tail + cell] = value
    courant = row(p.courant_at + p.full)
    for way in range(2):
        for r in range(p.part_rows):
            at = group * p.part_rows + (way * cells + r)
            c = jnp.take_along_axis(courant, at, axis=1)
            set_faces(tail_faces + way * p.part_rows + r, c)

    def sweep(at, faces_at, step, length, up, down):
        cell = [at + step * i for i in range(length)]
        face = [faces_at + step * i for i in range(length)]
        q = [q_ref[cell[i]] for i in range(length)]
        ext = [up(q[length - 1])] + q + [down(q[0]), down(q[1])]
        edge = [
            7.0 * (ext[i + 1] + ext[i + 2]) - (ext[i] + ext[i + 3]) for i in range(length)
        ]
        edges = [up(edge[length - 1])] + edge + [down(edge[0])]
        flux = []
        for i in range(length):
            near = near_ref[face[i]]
            upwind = near >= 0.0
            far = jnp.where(upwind, edges[i], edges[i + 2])
            mid = jnp.where(upwind, ext[i + 1], ext[i + 2])
            flux.append(near * edge[i] + far_ref[face[i]] * far + mid_ref[face[i]] * mid)
        fluxes = [up(flux[length - 1])] + flux
        for i in range(length):
            q_ref[cell[i]] = q[i] - (fluxes[i + 1] - fluxes[i])

    def low_tile(shift):
        return lambda v: pltpu.roll(v, shift, 0)

    def high_tile(shift):
        return lambda v: pltpu.roll(v, tiles - shift, 0)

    def low_group(v):
        moved = pltpu.roll(v, p.width, 1)
        return jnp.where(group == 0, low_tile(stride)(moved), moved)

    def high_group(v):
        moved = pltpu.roll(v, LANES - p.width, 1)
        return jnp.where(group == p.groups - 1, high_tile(stride)(moved), moved)

    def step(count, carry):
        for j in range(side):
            for kind in range(p.full):
                at, faces_at = kind * cells + j, kind * 2 * cells + j
                sweep(at, faces_at, side, side, low_tile(stride), high_tile(stride))
            sweep(tail + j, tail_faces + j, side, tall, low_group, high_group)
        for i in range(side):
            for kind in range(p.full):
                at, faces_at = kind * cells + i * side, (kind * 2 + 1) * cells + i * side
                sweep(at, faces_at, 1, side, low_tile(1), high_tile(1))
            if i < tall:
                at, faces_at = tail + i * side, tail_faces + p.part_rows + i * side
                sweep(at, faces_at, 1, side, low_tile(1), high_tile(1))
        return carry

    lax.fori_loop(0, SUBSTEPS, step, 0)

    pitch = p.layers * p.back_rows

    def send(layer, at, value):
        out_ref[pl.ds(layer * p.back_rows + at, tiles, stride=pitch), :] = value

    for kind in range(p.full):
        for cell, value in mirrored(
            lambda i, j: q_ref[kind * cells + i * side + j], side, plain
        ):
            layer, own = divmod(cell, p.own_cells)
            send(layer, kind * p.own_cells + own, value)
    rest = dict(mirrored(lambda i, j: q_ref[tail + i * side + j], tall, reversed_groups))
    for layer in range(p.layers):
        for r in range(p.back_part):
            rows = None
            for m in range(p.groups):
                at, source = divmod(
                    layer * p.own_cells + m * p.back_part + r, p.part_rows
                )[::-1]
                shift = (m - source) * p.width % LANES
                moved = pltpu.roll(rest[at], shift, 1) if shift else rest[at]
                rows = moved if rows is None else jnp.where(group == m, moved, rows)
            send(layer, p.back_tail + r, rows)


def mix_kernel(p, in_ref, weights_ref, *refs):
    out_refs, (x_ref, all_ref) = refs[: p.layers], refs[p.layers :]
    tiles = p.tiles
    in_ref = in_ref.reshape(tiles * p.layers * p.back_rows, LANES)
    shape = (tiles, LANES)
    pitch = p.layers * p.back_rows
    group = lane_group(shape, p.width)
    part = lax.broadcasted_iota(jnp.int32, shape, 0) % p.groups
    places = [(group == g) & (part == g) for g in range(p.groups)]

    def row(layer, at):
        return in_ref[pl.ds(layer * p.back_rows + at, tiles, stride=pitch), :]

    def mix(own):
        x = x_ref[own]
        weights = weights_ref[own]
        scale = 0.4 / jnp.sum(weights, axis=-1, keepdims=True)
        x_high = x.astype(jnp.bfloat16)
        x_low = (x - x_high.astype(jnp.float32)).astype(jnp.bfloat16)
        w_high = weights.astype(jnp.bfloat16)
        w_low = (weights - w_high.astype(jnp.float32)).astype(jnp.bfloat16)
        dot = functools.partial(jnp.dot, preferred_element_type=jnp.float32)
        both = dot(w_high, jnp.concatenate([x_high, x_low], axis=1))
        total = both[:, :LANES] + (both[:, LANES:] + dot(w_low, x_high))
        all_ref[pl.ds(own, p.all_levels, stride=p.own_cells), :] = 0.6 * x + scale * total

    for r in range(p.back_part):
        turned = []
        for layer in range(p.layers):
            value = row(layer, p.back_tail + r)
            turned.append([value] + [pltpu.roll(value, s * p.width, 1) for s in range(1, p.groups)])
        for m in range(p.groups):
            own = m * p.back_part + r
            for layer in range(p.layers):
                base = layer * p.levels
                for f in range(p.full):
                    x_ref[own, pl.ds(base + f, tiles, stride=p.full), :] = row(
                        layer, f * p.own_cells + own
                    )
                tail = jnp.zeros(shape, jnp.float32)
                for g in range(p.groups):
                    tail = jnp.where(places[g], turned[layer][(g - m) % p.groups], tail)
                reach = 1
                while reach < p.groups:
                    tail = tail + pltpu.roll(tail, tiles - reach, 0)
                    reach *= 2
                for h in range(p.spare):
                    at = base + p.full * tiles + h
                    x_ref[own, at : at + 1, :] = tail[h * p.groups : h * p.groups + 1]
            mix(own)
    me = lax.axis_index("lev")
    size = p.levels * p.own_cells
    for s in range(p.layers):
        layer = lax.rem(me + s, p.layers)
        out_refs[s][...] = all_ref[pl.ds(pl.multiple_of(layer * size, SUBLANES), size), :]


def place_kernel(p, shifts, *refs):
    in_refs, out_ref, sems = refs[: len(shifts)], refs[-2], refs[-1]
    me = lax.axis_index("lev")
    tall = p.own_cells // p.side
    copies = []
    for n, s in enumerate(shifts):
        layer = lax.rem(me - s + p.layers, p.layers)
        piece = in_refs[n].reshape(p.levels, tall, p.side, LANES)
        for r in range(tall):
            copies.append(
                pltpu.make_async_copy(
                    piece.at[:, r], out_ref.at[layer * tall + r], sems.at[len(copies)]
                )
            )
            copies[-1].start()
    for copy in copies:
        copy.wait()


def in_vmem(count):
    return [pl.BlockSpec(memory_space=pltpu.VMEM)] * count


def params():
    return pltpu.CompilerParams(vmem_limit_bytes=VMEM_LIMIT)


def by_levels(p, tracers, courant_first, courant_second, weights, frame_flip):
    f32 = jnp.float32
    across = (p.side, p.levels, p.side, p.tracers)
    chips = p.tiles // 2
    blocks = (p.rows // p.side, p.side, LANES)
    *own, other = pl.pallas_call(
        functools.partial(pack_kernel, p),
        out_shape=[jax.ShapeDtypeStruct(blocks, f32)] * chips
        + [jax.ShapeDtypeStruct((chips,) + blocks, f32)],
        in_specs=[pl.BlockSpec(memory_space=pltpu.HBM)] * 4,
        out_specs=in_vmem(chips + 1),
        scratch_shapes=[
            pltpu.VMEM((p.side, p.spare, p.side, LANES), f32),
            pltpu.VMEM((2, p.side, p.side, p.levels), f32),
            pltpu.VMEM((1, 2), jnp.int32),
            pltpu.VMEM((LANES, LANES), f32),
            pltpu.VMEM((p.tiles, p.part_rows // p.side + 1, p.side, LANES), f32),
            pltpu.SemaphoreType.DMA((4 + p.tiles,)),
        ],
        compiler_params=params(),
        name="pack",
    )(
        *(
            pltpu.with_memory_space_constraint(value, pltpu.HBM)
            for value in (
                tracers[0].transpose(0, 2, 1, 3),
                courant_first[0],
                courant_second[0],
                frame_flip,
            )
        )
    )
    got = swapped(other, "tile", 1)
    pieces = [None] * p.tiles
    for s in range(chips - 1, -1, -1):
        for e, block in ((0, own[s]), (1, got[s])):
            block = block.reshape(p.rows, LANES)
            pieces[2 * s + e] = swapped(block, "tile", 2 * s) if s else block
    moved = pl.pallas_call(
        functools.partial(advect_kernel, p, tile_stride(p.tiles)),
        out_shape=jax.ShapeDtypeStruct(
            (p.tiles * p.layers, p.back_rows // FEW, FEW, LANES), f32
        ),
        in_specs=in_vmem(len(pieces)),
        out_specs=pl.BlockSpec(memory_space=pltpu.VMEM),
        scratch_shapes=[
            pltpu.VMEM((p.tiles * p.rows, LANES), f32),
            pltpu.VMEM((p.full * p.cells + p.part_rows, p.tiles, LANES), f32),
        ]
        + [pltpu.VMEM((2 * (p.full * p.cells + p.part_rows), p.tiles, LANES), f32)] * 3,
        compiler_params=params(),
        name="advect",
    )(*pieces)
    columns = lax.all_to_all(
        moved,
        ("tile", "lev"),
        split_axis=0,
        concat_axis=0,
        tiled=True,
    )
    size = p.levels * p.own_cells
    mixed = pl.pallas_call(
        functools.partial(mix_kernel, p),
        out_shape=[jax.ShapeDtypeStruct((size, LANES), f32)] * p.layers,
        in_specs=in_vmem(2),
        out_specs=in_vmem(p.layers),
        scratch_shapes=[
            pltpu.VMEM((p.own_cells, p.all_levels, LANES), f32),
            pltpu.VMEM((p.all_levels * p.own_cells, LANES), f32),
        ],
        compiler_params=params(),
        name="mix",
    )(
        columns,
        weights.reshape(p.own_cells, p.all_levels, p.all_levels),
    )
    pieces = [mixed[0]] + [passed_along(mixed[s], "lev", s) for s in range(1, p.layers)]
    order = sorted(range(p.layers), key=lambda s: -min(s, p.layers - s) if s else -p.layers)
    placed = None
    for shifts in (order[:2], order[2:]):
        before = [] if placed is None else [placed]
        placed = pl.pallas_call(
            functools.partial(place_kernel, p, shifts),
            out_shape=jax.ShapeDtypeStruct(across, f32),
            in_specs=in_vmem(len(shifts))
            + [pl.BlockSpec(memory_space=pltpu.HBM)] * len(before),
            out_specs=pl.BlockSpec(memory_space=pltpu.HBM),
            scratch_shapes=[
                pltpu.SemaphoreType.DMA((len(shifts) * p.own_cells // p.side,))
            ],
            input_output_aliases={len(shifts): 0} if before else {},
            compiler_params=params(),
            name="place",
        )(*(pieces[s] for s in shifts), *before)
    return placed.transpose(0, 2, 1, 3)[None]


def on_device(tracers, courant_first, courant_second, weights, frame_flip):
    plan = Plan(
        tracers.shape[1],
        tracers.shape[3],
        tracers.shape[4],
        lax.axis_size("tile"),
        lax.axis_size("lev"),
    )
    if tracers.shape[1] == tracers.shape[2] and tracers.shape[0] == 1 and plan.fits:
        return by_levels(plan, tracers, courant_first, courant_second, weights, frame_flip)
    return by_halos(tracers, courant_first, courant_second, weights, frame_flip)


def solution(mesh):
    in_specs = (
        P("tile", None, None, "lev", None),
        P("tile", None, None, "lev"),
        P("tile", None, None, "lev"),
        P("tile", "lev", None, None, None),
        P("tile", None),
    )
    out_specs = P("tile", None, None, "lev", None)
    return jax.shard_map(
        on_device, mesh=mesh, in_specs=in_specs, out_specs=out_specs, check_vma=False
    )
```
